128 devices in a mesh: grid: 16 (over z, x_lo, core), vec: 8 (over x_hi, y).
Axes of the slice: x: 4 (x_hi: 2, x_lo: 2; x = x_hi * 2 + x_lo), y: 4, z: 4, core: 2. Of those that a mesh axis runs over, the one named last changes fastest.
Arguments:
- orbitals: bfloat16 [884736, 512], P(('grid', 'vec')), may hold values from -1.296875 to 1.296875
- inverse_panel: bfloat16 [2048, 64], replicated, may hold values from -0.125 to 0.125
- points: int32 [2048], replicated, may hold values from 0 to 884735, as said below
Outputs:
- projected: float32 [2048, 64], P(('grid', 'vec'))
The draws below stay inside these ranges and needn't reach their ends.
Inputs may be any that keep to these rules, and one draw needn't show every extreme that they name: `points`: distinct cell indices.
All inputs are finite; a program needn't handle non-finite values.
Results may differ from the reference program's by a relative error of at most 0.005.
Values may be sent and summed in bfloat16 or wider, within the bound.
No kernel may reach another device: no remote copies, remote signals or barrier semaphores. Data moves between devices by JAX's collectives and lax.ppermute only.
A program may use at most 128 MiB of HBM per device.

```python
import math
import jax
import jax.numpy as jnp
from jax import lax

NG = 96
NORB = 512
NPTS = 2048
COLS = 64


def draw_points(key, part):
    return jax.random.permutation(key, NG ** 3)[:NPTS].astype(jnp.int32)


def block_scale(stream_key, shape, cuts, least, high):
    level = 1.0
    for position, parts in cuts:
        draws = jax.random.uniform(jax.random.fold_in(jax.random.fold_in(stream_key, 6), position), (parts,), jnp.float32, least / len(cuts), high / len(cuts))
        level = level * jnp.repeat(jnp.exp(draws), shape[position] // parts).reshape((-1,) + (1,) * (len(shape) - 1 - position))
    return level


def normal_values(stream_key, dims, width, limit, shards=(), held_as=jnp.bfloat16):
    values = jax.random.normal(stream_key, dims, jnp.float32) * width
    if len(shards) > 0:
        values = block_scale(stream_key, dims, shards, -0.22, 0.18) * values
    return jnp.clip(values, min=-limit, max=limit).astype(held_as)


def setup_inputs(seed: int = 0) -> dict:
    seeds = jax.random.split(jax.random.key(seed), 4)
    return {
        "orbitals": normal_values(seeds[0], (NG**3, NORB), 0.21, 1.296875, ((0, 128),)),
        "inverse_panel": normal_values(seeds[1], (NPTS, COLS), NPTS ** -0.5, 0.125),
        "points": draw_points(jax.random.fold_in(seeds[3], 71), 0),
    }


SCREEN = 2.25

def wave_tables(count):
    index = lax.iota(jnp.int32, count)
    phase = index[:, None] * index[None, :] % count
    angle = phase.astype(jnp.float32) * (2.0 * math.pi / count)
    return (jnp.cos(angle).astype(jnp.bfloat16), jnp.sin(angle).astype(jnp.bfloat16))

def wavenumber(index, count):
    return jnp.where(index < count // 2, index, index - count).astype(jnp.float32)

def screened(wave_x, wave_y, wave_z):
    squared = wave_x[:, None, None] * wave_x[:, None, None] + wave_y[None, :, None] * wave_y[None, :, None] + wave_z[None, None, :] * wave_z[None, None, :]
    factor = NG / (2.0 * math.pi) * (NG / (2.0 * math.pi))
    return jnp.where(squared > 0.5, factor / (squared + SCREEN), jnp.float32(0.0))

def contract(data, table, form):
    return jnp.einsum(form, data.astype(jnp.float32), table.astype(jnp.float32))

def poisson(column, cos_tab, sin_tab, kernel):
    bf = jnp.bfloat16
    z_re = contract(column, cos_tab, 'xyz,zk->xyk').astype(bf)
    z_im = (-contract(column, sin_tab, 'xyz,zk->xyk')).astype(bf)
    y_re = (contract(z_re, cos_tab, 'xyz,yk->xkz') + contract(z_im, sin_tab, 'xyz,yk->xkz')).astype(bf)
    y_im = (contract(z_im, cos_tab, 'xyz,yk->xkz') - contract(z_re, sin_tab, 'xyz,yk->xkz')).astype(bf)
    x_re = contract(y_re, cos_tab, 'xyz,xk->kyz') + contract(y_im, sin_tab, 'xyz,xk->kyz')
    x_im = contract(y_im, cos_tab, 'xyz,xk->kyz') - contract(y_re, sin_tab, 'xyz,xk->kyz')
    q_re = (x_re * kernel).astype(bf)
    q_im = (x_im * kernel).astype(bf)
    i_re = (contract(q_re, cos_tab, 'xyz,xk->kyz') - contract(q_im, sin_tab, 'xyz,xk->kyz')).astype(bf)
    i_im = (contract(q_im, cos_tab, 'xyz,xk->kyz') + contract(q_re, sin_tab, 'xyz,xk->kyz')).astype(bf)
    h_re = (contract(i_re, cos_tab, 'xyz,yk->xkz') - contract(i_im, sin_tab, 'xyz,yk->xkz')).astype(bf)
    h_im = (contract(i_im, cos_tab, 'xyz,yk->xkz') + contract(i_re, sin_tab, 'xyz,yk->xkz')).astype(bf)
    final = contract(h_re, cos_tab, 'xyz,zk->xyk') - contract(h_im, sin_tab, 'xyz,zk->xyk')
    return (final / float(NG ** 3)).astype(bf)

def reference(orbitals, inverse_panel, points):
    point_rows = orbitals[points]
    blocks = orbitals.reshape(NG, NG * NG, NORB)

    def make_pair(block):
        correlation = jnp.dot(block, point_rows.T, preferred_element_type=jnp.float32)
        return (correlation * correlation).astype(jnp.bfloat16)

    def fit_block(block):
        return jnp.dot(make_pair(block), inverse_panel, preferred_element_type=jnp.float32).astype(jnp.bfloat16)
    fitted = lax.map(fit_block, blocks)
    field = jnp.moveaxis(fitted.reshape(NG, NG, NG, COLS), 3, 0)
    cos_tab, sin_tab = wave_tables(NG)
    waves = wavenumber(lax.iota(jnp.int32, NG), NG)
    kernel = screened(waves, waves, waves)
    potential = lax.map(lambda column: poisson(column, cos_tab, sin_tab, kernel), field)
    pot_blocks = jnp.moveaxis(potential.reshape(COLS, NG, NG * NG), 1, 0)

    def accumulate(total, pieces):
        block, pot_block = pieces
        pair = make_pair(block)
        term = lax.dot_general(pair, pot_block, (((0,), (1,)), ((), ())), preferred_element_type=jnp.float32)
        return (total + term, None)
    total, _ = lax.scan(accumulate, jnp.zeros((NPTS, COLS), jnp.float32), (blocks, pot_blocks))
    return total * jnp.float32(1.0 / math.sqrt(float(NG ** 3)))
```

```python
import math

import jax
import jax.numpy as jnp
from jax import lax
from jax.sharding import PartitionSpec as P

NG = 96
HALF = NG // 2
SCREEN = 2.25
BOTH = ("grid", "vec")


def wave_tables(count):
    index = lax.iota(jnp.int32, count)
    phase = index[:, None] * index[None, :] % count
    angle = phase.astype(jnp.float32) * (2.0 * math.pi / count)
    return (jnp.cos(angle).astype(jnp.bfloat16), jnp.sin(angle).astype(jnp.bfloat16))


def real_basis():
    cos_tab, sin_tab = wave_tables(NG)
    return jnp.concatenate([cos_tab[:, : HALF + 1], sin_tab[:, 1:HALF]], axis=1)


def wave_of(column):
    return jnp.where(column <= HALF, column, column - HALF)


def weight_of(wave):
    return jnp.where((wave == 0) | (wave == HALF), 1.0, 2.0).astype(jnp.float32)


def shards(orbitals, inverse_panel, points):
    bf = jnp.bfloat16
    f32 = jnp.float32
    row_count = orbitals.shape[0]
    vec_count = lax.axis_size("vec")
    devices = lax.axis_size("grid") * vec_count
    me = lax.axis_index("grid") * vec_count + lax.axis_index("vec")
    npoints = points.shape[0]
    local_pos = points - me * row_count
    inside = (local_pos >= 0) & (local_pos < row_count)
    picked = jnp.take(orbitals, jnp.clip(local_pos, 0, row_count - 1), axis=0)
    picked = jnp.where(inside[:, None], picked, jnp.zeros_like(picked)).astype(f32)
    point_rows = lax.psum(picked, BOTH).astype(bf)

    def pair_block(block):
        correlation = lax.dot_general(
            block, point_rows, (((1,), (1,)), ((), ())), preferred_element_type=f32
        )
        return (correlation * correlation).astype(bf)

    pair = lax.map(pair_block, orbitals.reshape(4, row_count // 4, orbitals.shape[1])).reshape(
        row_count, npoints
    )
    cols = inverse_panel.shape[1]
    fit = jnp.dot(pair, inverse_panel, preferred_element_type=f32).astype(bf)
    basis = real_basis()
    lines = row_count // NG
    field = fit.reshape(lines, NG, cols)
    spec_z = jnp.einsum("yzc,zm->ymc", field, basis, preferred_element_type=f32).astype(bf)
    send = spec_z.reshape(lines // 8, 8, 32, 3, 4, 16).transpose(2, 4, 0, 3, 1, 5)
    send = send.reshape(devices, lines // 8 * 3, 128)
    planes = lax.all_to_all(send, BOTH, 0, 0)
    planes = planes.reshape(NG, NG // 8, 3, 8, 16).transpose(2, 4, 0, 1, 3).reshape(48, NG, NG)
    spec_y = jnp.einsum("pxy,yk->pxk", planes, basis, preferred_element_type=f32).astype(bf)
    spec_x = jnp.einsum("pxk,xl->plk", spec_y, basis, preferred_element_type=f32)
    wave = wave_of(lax.iota(jnp.int32, NG))
    wave_z = wave_of((me // 4) * 3 + lax.iota(jnp.int32, 3))
    wf = wave.astype(f32)
    wz = wave_z.astype(f32)
    squared = (wf * wf)[None, :, None] + (wf * wf)[None, None, :] + (wz * wz)[:, None, None]
    factor = NG / (2.0 * math.pi) * (NG / (2.0 * math.pi))
    kernel = jnp.where(squared > 0.5, factor / (squared + SCREEN), jnp.float32(0.0))
    weight = weight_of(wave)
    kernel = kernel * (
        weight[None, :, None] * weight[None, None, :] * weight_of(wave_z)[:, None, None]
    )
    scaled = (spec_x.reshape(3, 16, NG, NG) * kernel[:, None]).astype(bf).reshape(48, NG, NG)
    back_x = jnp.einsum("plk,xl->pxk", scaled, basis, preferred_element_type=f32).astype(bf)
    back_y = jnp.einsum("pxk,yk->pxy", back_x, basis, preferred_element_type=f32).astype(bf)
    ret = back_y.reshape(3, 16, NG, NG // 8, 8).transpose(2, 3, 0, 4, 1)
    ret = ret.reshape(devices, lines // 8 * 3, 128)
    got = lax.all_to_all(ret, BOTH, 0, 0)
    got = got.reshape(32, 4, lines // 8, 3, 8, 16).transpose(2, 4, 0, 3, 1, 5)
    got = got.reshape(lines, NG, cols)
    final = jnp.einsum("ymc,zm->yzc", got, basis, preferred_element_type=f32)
    potential = (final / float(NG**3)).astype(bf).reshape(row_count, cols)
    term = lax.dot_general(
        pair, potential, (((0,), (0,)), ((), ())), preferred_element_type=f32
    )
    scale = 1.0 / math.sqrt(float(NG**3))
    parts = (term * f32(scale)).reshape(devices, 8, 128)
    parts = lax.all_to_all(parts, BOTH, 0, 0)
    return jnp.sum(parts, axis=0).reshape(npoints // devices, cols)


def solution(mesh):
    in_specs = (P(BOTH, None), P(), P())
    return jax.shard_map(
        shards, mesh=mesh, in_specs=in_specs, out_specs=P(BOTH, None), check_vma=False
    )
```

```python
import functools
import math

import jax
import jax.numpy as jnp
import numpy as np
from jax import lax
from jax.experimental import pallas as pl
from jax.experimental.pallas import tpu as pltpu
from jax.sharding import PartitionSpec as P

NG = 96
HALF = NG // 2
SCREEN = 2.25
BOTH = ("grid", "vec")
BF = jnp.bfloat16
F32 = jnp.float32

LINES = 72
OCT = LINES // 8
MG, MI = 32, 3
CG, CI = 4, 16
ROWS = 32
CELLS = 8 * NG


def basis_table():
    index = np.arange(NG)
    phase = (index[:, None] * index[None, :]) % NG
    angle = phase.astype(np.float32) * np.float32(2.0 * math.pi / NG)
    cos_tab = np.cos(angle).astype(BF).astype(np.float32)
    sin_tab = np.sin(angle).astype(BF).astype(np.float32)
    return np.concatenate([cos_tab[:, : HALF + 1], sin_tab[:, 1:HALF]], axis=1)


def tables():
    basis = basis_table()
    ahead = np.zeros((MG, ROWS, OCT, NG), np.float32)
    for octet in range(OCT):
        for mi in range(MI):
            ahead[:, octet * MI + mi, octet, :] = basis[:, mi::MI].T
    ahead = ahead.reshape(MG * ROWS, OCT * NG)
    lane = np.arange(512).reshape(8, CG, CI)
    order = lane.transpose(1, 0, 2).reshape(-1)
    swap = np.zeros((512, 512), np.float32)
    swap[order, np.arange(512)] = 1.0
    wide = np.kron(basis, np.eye(CI, dtype=np.float32))
    x_order = (3 * np.arange(32)[None, :] + np.arange(3)[:, None]).reshape(-1)
    x_basis = basis[x_order]
    return {
        "ahead": ahead,
        "back": ahead.T,
        "swap": swap,
        "unswap": swap.T,
        "wide": wide,
        "wide_t": wide.T,
        "x_ahead": x_basis.T,
        "x_back": x_basis,
    }


def const(array):
    return jnp.asarray(np.ascontiguousarray(array).astype(BF))


def mm(a, b):
    return jnp.dot(a, b, preferred_element_type=F32)


def pair_kernel(orb, rows_t, panel, ahead, swap, pair, send, fit):
    step = pl.program_id(0)
    npts = rows_t.shape[1]
    chunk = 512
    total = jnp.zeros((CELLS, 128), F32)
    for start in range(0, npts, chunk):
        corr = mm(orb[...], rows_t[:, start : start + chunk])
        block = (corr * corr).astype(BF)
        pair[:, start : start + chunk] = block
        total = total + mm(block, panel[start : start + chunk, :])
    low = lax.broadcasted_iota(jnp.int32, (NG, 128), 1) < 64
    for two in range(4):
        even = total[2 * two * NG : (2 * two + 1) * NG]
        odd = total[(2 * two + 1) * NG : (2 * two + 2) * NG]
        fit[pl.ds(pl.multiple_of(step * NG, NG), NG), two * 128 : (two + 1) * 128] = jnp.where(
            low, even, odd
        ).astype(BF)

    @pl.when(step == pl.num_programs(0) - 1)
    def _():
        for part in range(4):
            rows = MG * ROWS // 4
            spec = mm(ahead[part * rows : (part + 1) * rows, :], fit[...]).astype(BF)
            moved = mm(spec, swap[...]).astype(BF)
            for cg in range(CG):
                send[part * MG // 4 : (part + 1) * MG // 4, cg] = moved[
                    :, cg * 128 : (cg + 1) * 128
                ].reshape(MG // 4, ROWS, 128)


def make_pairs(orbitals, rows_t, panel2, tab):
    npts = rows_t.shape[1]
    norb = orbitals.shape[1]
    steps = orbitals.shape[0] // CELLS
    whole = lambda shape: pl.BlockSpec(shape, lambda i: (0,) * len(shape))
    return pl.pallas_call(
        pair_kernel,
        grid=(steps,),
        in_specs=[
            pl.BlockSpec((CELLS, norb), lambda i: (i, 0)),
            whole(rows_t.shape),
            whole(panel2.shape),
            whole(tab["ahead"].shape),
            whole(tab["swap"].shape),
        ],
        out_specs=[
            pl.BlockSpec((CELLS, npts), lambda i: (i, 0)),
            whole((MG, CG, ROWS, 128)),
        ],
        out_shape=[
            jax.ShapeDtypeStruct((orbitals.shape[0], npts), BF),
            jax.ShapeDtypeStruct((MG, CG, ROWS, 128), BF),
        ],
        scratch_shapes=[pltpu.VMEM((OCT * NG, 512), BF)],
        compiler_params=pltpu.CompilerParams(vmem_limit_bytes=48 * 2**20),
        name="pairs",
    )(orbitals, rows_t, panel2, const(tab["ahead"]), const(tab["swap"]))


def places():
    for part in range(4):
        for octet in range(OCT):
            for mi in range(MI):
                spot = part * OCT + octet
                yield part * ROWS + octet * MI + mi, mi, spot // 12, spot % 12


def solve_kernel(first, got, wide, wide_t, x_ahead, x_back, out, flat, field):
    flat[...] = got[...].astype(F32)
    for row, mi, xr, yo in places():
        field[mi, xr * 32 : (xr + 1) * 32, yo * 128 : (yo + 1) * 128] = flat[
            pl.ds(row, 32, stride=4 * ROWS), :
        ].astype(BF)
    lane = lax.broadcasted_iota(jnp.int32, (1, NG * CI), 1) // CI
    subl = lax.broadcasted_iota(jnp.int32, (NG, 1), 0)
    wave_of = lambda k: jnp.where(k <= HALF, k, k - HALF)
    weight = lambda w: jnp.where((w == 0) | (w == HALF), 1.0, 2.0).astype(F32)
    wave_y, wave_x = wave_of(lane), wave_of(subl)
    square = lambda w: w.astype(F32) * w.astype(F32)
    factor = NG / (2.0 * math.pi) * (NG / (2.0 * math.pi))
    flat[...] = jnp.zeros_like(flat)
    spec_y = mm(field[...].reshape(MI * NG, NG * CI), wide[...]).astype(BF)
    backs = []
    for mi in range(MI):
        wave_z = wave_of(first[0] + mi)
        spec = mm(x_ahead[...], spec_y[mi * NG : (mi + 1) * NG])
        total = square(wave_x) + square(wave_y) + square(wave_z)
        gain = weight(wave_x) * (weight(wave_y) * weight(wave_z))
        kernel = jnp.where(total > 0.5, factor / (total + SCREEN), 0.0) * gain
        scaled = (spec * kernel).astype(BF)
        backs.append(mm(x_back[...], scaled).astype(BF))
    plane = mm(jnp.concatenate(backs, axis=0), wide_t[...])
    for row, mi, xr, yo in places():
        flat[pl.ds(row, 32, stride=4 * ROWS), :] = plane[
            mi * NG + xr * 32 : mi * NG + (xr + 1) * 32, yo * 128 : (yo + 1) * 128
        ]
    out[...] = flat[...].astype(BF)


def solve(first, got, tab):
    vmem = pl.BlockSpec(memory_space=pltpu.VMEM)
    return pl.pallas_call(
        solve_kernel,
        in_specs=[pl.BlockSpec(memory_space=pltpu.SMEM)] + [vmem] * 5,
        out_specs=vmem,
        out_shape=jax.ShapeDtypeStruct(got.shape, BF),
        scratch_shapes=[
            pltpu.VMEM(got.shape, F32),
            pltpu.VMEM((MI, NG, NG * CI), BF),
        ],
        compiler_params=pltpu.CompilerParams(vmem_limit_bytes=48 * 2**20),
        name="solve",
    )(
        first,
        got,
        const(tab["wide"]),
        const(tab["wide_t"]),
        const(tab["x_ahead"]),
        const(tab["x_back"]),
    )


def project_kernel(got, unswap, back, pair, out, spec, pot, acc):
    step = pl.program_id(0)

    @pl.when(step == 0)
    def _():
        for part in range(4):
            rows = MG * ROWS // 4
            block = jnp.concatenate(
                [
                    got[part * MG // 4 : (part + 1) * MG // 4, cg].reshape(rows, 128)
                    for cg in range(CG)
                ],
                axis=1,
            )
            spec[part * rows : (part + 1) * rows, :] = mm(block, unswap[...]).astype(BF)
        for octet in range(OCT):
            final = mm(back[octet * NG : (octet + 1) * NG, :], spec[...])
            final = final / float(NG**3)
            for yi in range(8):
                start = (octet * 8 + yi) * NG
                pot[start : start + NG, :] = final[:, yi * 64 : (yi + 1) * 64].astype(BF)
        acc[...] = jnp.zeros_like(acc)

    block = pot[pl.ds(pl.multiple_of(step * CELLS, CELLS), CELLS), :]
    acc[...] += lax.dot_general(
        block, pair[...], (((0,), (0,)), ((), ())), preferred_element_type=F32
    )

    @pl.when(step == pl.num_programs(0) - 1)
    def _():
        scale = 1.0 / math.sqrt(float(NG**3))
        turned = (acc[...] * scale).T.reshape(128, 2, 8, 64)
        out[...] = jnp.concatenate([turned[:, 0], turned[:, 1]], axis=-1)


def project(got, pair, tab):
    steps = pair.shape[0] // CELLS
    whole = lambda shape: pl.BlockSpec(shape, lambda i: (0,) * len(shape))
    return pl.pallas_call(
        project_kernel,
        grid=(steps,),
        in_specs=[
            whole(got.shape),
            whole(tab["unswap"].shape),
            whole(tab["back"].shape),
            pl.BlockSpec((CELLS, pair.shape[1]), lambda i: (i, 0)),
        ],
        out_specs=whole((128, 8, 128)),
        out_shape=jax.ShapeDtypeStruct((128, 8, 128), F32),
        scratch_shapes=[
            pltpu.VMEM((MG * ROWS, 512), BF),
            pltpu.VMEM((pair.shape[0], 64), BF),
            pltpu.VMEM((64, pair.shape[1]), F32),
        ],
        compiler_params=pltpu.CompilerParams(vmem_limit_bytes=48 * 2**20),
        name="project",
    )(got, const(tab["unswap"]), const(tab["back"]), pair)


def gather_rows(orbitals, points, me):
    row_count = orbitals.shape[0]
    local_pos = points - me * row_count
    inside = (local_pos >= 0) & (local_pos < row_count)
    picked = jnp.take(orbitals, jnp.clip(local_pos, 0, row_count - 1), axis=0)
    picked = jnp.where(inside[:, None], picked, jnp.zeros_like(picked)).astype(F32)
    return lax.psum(picked, BOTH).astype(BF)


def shards(orbitals, inverse_panel, points):
    tab = tables()
    vec_count = lax.axis_size("vec")
    devices = lax.axis_size("grid") * vec_count
    me = lax.axis_index("grid") * vec_count + lax.axis_index("vec")
    npoints, cols = inverse_panel.shape
    rows_t = gather_rows(orbitals, points, me).T
    panel2 = jnp.concatenate([inverse_panel, inverse_panel], axis=1)
    pair, send = make_pairs(orbitals, rows_t, panel2, tab)
    planes = lax.all_to_all(send.reshape(devices, ROWS, 128), BOTH, 0, 0)
    first = (me // CG * MI).astype(jnp.int32).reshape(1)
    ret = solve(first, planes.reshape(devices * ROWS, 128), tab)
    got = lax.all_to_all(ret.reshape(devices, ROWS, 128), BOTH, 0, 0)
    parts = project(got.reshape(MG, CG, ROWS, 128), pair, tab)
    parts = lax.all_to_all(parts, BOTH, 0, 0)
    total = jnp.sum(parts, axis=0)
    return jnp.concatenate([total[:, :cols], total[:, cols:]], axis=0)


def solution(mesh):
    in_specs = (P(BOTH, None), P(), P())
    return jax.shard_map(
        shards, mesh=mesh, in_specs=in_specs, out_specs=P(BOTH, None), check_vma=False
    )
```

```python
import functools
import math

import jax
import jax.numpy as jnp
import numpy as np
from jax import lax
from jax.experimental import pallas as pl
from jax.experimental.pallas import tpu as pltpu
from jax.sharding import PartitionSpec as P

NG = 96
HALF = NG // 2
SCREEN = 2.25
BOTH = ("grid", "vec")
BF = jnp.bfloat16
F32 = jnp.float32

LINES = 72
OCT = LINES // 8
MG, MI = 32, 3
CG, CI = 4, 16
ROWS = 32
CELLS = 8 * NG


def basis_table():
    index = np.arange(NG)
    phase = (index[:, None] * index[None, :]) % NG
    angle = phase.astype(np.float32) * np.float32(2.0 * math.pi / NG)
    cos_tab = np.cos(angle).astype(BF).astype(np.float32)
    sin_tab = np.sin(angle).astype(BF).astype(np.float32)
    return np.concatenate([cos_tab[:, : HALF + 1], sin_tab[:, 1:HALF]], axis=1)


def tables():
    basis = basis_table()
    ahead = np.zeros((MG, ROWS, OCT, NG), np.float32)
    for octet in range(OCT):
        for mi in range(MI):
            ahead[:, octet * MI + mi, octet, :] = basis[:, mi::MI].T
    ahead = ahead.reshape(MG * ROWS, OCT * NG)
    lane = np.arange(512).reshape(8, CG, CI)
    order = lane.transpose(1, 0, 2).reshape(-1)
    swap = np.zeros((512, 512), np.float32)
    swap[order, np.arange(512)] = 1.0
    wide = np.kron(basis, np.eye(CI, dtype=np.float32))
    x_order = (3 * np.arange(32)[None, :] + np.arange(3)[:, None]).reshape(-1)
    x_basis = basis[x_order]
    return {
        "ahead": ahead,
        "back": ahead.T,
        "swap": swap,
        "unswap": swap.T,
        "wide": wide,
        "wide_t": wide.T,
        "x_ahead": x_basis.T,
        "x_back": x_basis,
    }


def const(array):
    return jnp.asarray(np.ascontiguousarray(array).astype(BF))


def mm(a, b):
    return jnp.dot(a, b, preferred_element_type=F32)


def pair_kernel(orb, rows_t, panel, ahead, swap, pair, send, fit):
    step = pl.program_id(0)
    npts = rows_t.shape[1]
    chunk = 512
    total = jnp.zeros((CELLS, 128), F32)
    for start in range(0, npts, chunk):
        corr = mm(orb[...], rows_t[:, start : start + chunk])
        block = (corr * corr).astype(BF)
        pair[:, start : start + chunk] = block
        total = total + mm(block, panel[start : start + chunk, :])
    low = lax.broadcasted_iota(jnp.int32, (NG, 128), 1) < 64
    for two in range(4):
        even = total[2 * two * NG : (2 * two + 1) * NG]
        odd = total[(2 * two + 1) * NG : (2 * two + 2) * NG]
        fit[pl.ds(pl.multiple_of(step * NG, NG), NG), two * 128 : (two + 1) * 128] = jnp.where(
            low, even, odd
        ).astype(BF)

    @pl.when(step == pl.num_programs(0) - 1)
    def _():
        for part in range(4):
            rows = MG * ROWS // 4
            spec = mm(ahead[part * rows : (part + 1) * rows, :], fit[...]).astype(BF)
            moved = mm(spec, swap[...]).astype(BF)
            for cg in range(CG):
                send[part * MG // 4 : (part + 1) * MG // 4, cg] = moved[
                    :, cg * 128 : (cg + 1) * 128
                ].reshape(MG // 4, ROWS, 128)


def make_pairs(orbitals, rows_t, panel2, tab):
    npts = rows_t.shape[1]
    norb = orbitals.shape[1]
    steps = orbitals.shape[0] // CELLS
    whole = lambda shape: pl.BlockSpec(shape, lambda i: (0,) * len(shape))
    return pl.pallas_call(
        pair_kernel,
        grid=(steps,),
        in_specs=[
            pl.BlockSpec((CELLS, norb), lambda i: (i, 0)),
            whole(rows_t.shape),
            whole(panel2.shape),
            whole(tab["ahead"].shape),
            whole(tab["swap"].shape),
        ],
        out_specs=[
            pl.BlockSpec((CELLS, npts), lambda i: (i, 0)),
            whole((MG, CG, ROWS, 128)),
        ],
        out_shape=[
            jax.ShapeDtypeStruct((orbitals.shape[0], npts), BF),
            jax.ShapeDtypeStruct((MG, CG, ROWS, 128), BF),
        ],
        scratch_shapes=[pltpu.VMEM((OCT * NG, 512), BF)],
        compiler_params=pltpu.CompilerParams(vmem_limit_bytes=48 * 2**20),
        name="pairs",
    )(orbitals, rows_t, panel2, const(tab["ahead"]), const(tab["swap"]))


def places():
    for part in range(4):
        for octet in range(OCT):
            for mi in range(MI):
                spot = part * OCT + octet
                yield part * ROWS + octet * MI + mi, mi, spot // 12, spot % 12


def solve_kernel(first, got, wide, wide_t, x_ahead, x_back, out, flat, field):
    flat[...] = got[...].astype(F32)
    for row, mi, xr, yo in places():
        field[mi, xr * 32 : (xr + 1) * 32, yo * 128 : (yo + 1) * 128] = flat[
            pl.ds(row, 32, stride=4 * ROWS), :
        ].astype(BF)
    lane = lax.broadcasted_iota(jnp.int32, (1, NG * CI), 1) // CI
    subl = lax.broadcasted_iota(jnp.int32, (NG, 1), 0)
    wave_of = lambda k: jnp.where(k <= HALF, k, k - HALF)
    weight = lambda w: jnp.where((w == 0) | (w == HALF), 1.0, 2.0).astype(F32)
    wave_y, wave_x = wave_of(lane), wave_of(subl)
    square = lambda w: w.astype(F32) * w.astype(F32)
    factor = NG / (2.0 * math.pi) * (NG / (2.0 * math.pi))
    flat[...] = jnp.zeros_like(flat)
    spec_y = mm(field[...].reshape(MI * NG, NG * CI), wide[...]).astype(BF)
    backs = []
    for mi in range(MI):
        wave_z = wave_of(first[0] + mi)
        spec = mm(x_ahead[...], spec_y[mi * NG : (mi + 1) * NG])
        total = square(wave_x) + square(wave_y) + square(wave_z)
        gain = weight(wave_x) * (weight(wave_y) * weight(wave_z))
        kernel = jnp.where(total > 0.5, factor / (total + SCREEN), 0.0) * gain
        scaled = (spec * kernel).astype(BF)
        backs.append(mm(x_back[...], scaled).astype(BF))
    plane = mm(jnp.concatenate(backs, axis=0), wide_t[...])
    for row, mi, xr, yo in places():
        flat[pl.ds(row, 32, stride=4 * ROWS), :] = plane[
            mi * NG + xr * 32 : mi * NG + (xr + 1) * 32, yo * 128 : (yo + 1) * 128
        ]
    out[...] = flat[...].astype(BF)


def solve(first, got, tab):
    vmem = pl.BlockSpec(memory_space=pltpu.VMEM)
    return pl.pallas_call(
        solve_kernel,
        in_specs=[pl.BlockSpec(memory_space=pltpu.SMEM)] + [vmem] * 5,
        out_specs=vmem,
        out_shape=jax.ShapeDtypeStruct(got.shape, BF),
        scratch_shapes=[
            pltpu.VMEM(got.shape, F32),
            pltpu.VMEM((MI, NG, NG * CI), BF),
        ],
        compiler_params=pltpu.CompilerParams(vmem_limit_bytes=48 * 2**20),
        name="solve",
    )(
        first,
        got,
        const(tab["wide"]),
        const(tab["wide_t"]),
        const(tab["x_ahead"]),
        const(tab["x_back"]),
    )


def project_kernel(got, unswap, back, pair, out, spec, pot, acc):
    step = pl.program_id(0)

    @pl.when(step == 0)
    def _():
        for part in range(4):
            rows = MG * ROWS // 4
            block = jnp.concatenate(
                [
                    got[part * MG // 4 : (part + 1) * MG // 4, cg].reshape(rows, 128)
                    for cg in range(CG)
                ],
                axis=1,
            )
            spec[part * rows : (part + 1) * rows, :] = mm(block, unswap[...]).astype(BF)
        for octet in range(OCT):
            final = mm(back[octet * NG : (octet + 1) * NG, :], spec[...])
            final = final / float(NG**3)
            for yi in range(8):
                start = (octet * 8 + yi) * NG
                pot[start : start + NG, :] = final[:, yi * 64 : (yi + 1) * 64].astype(BF)
        acc[...] = jnp.zeros_like(acc)

    block = pot[pl.ds(pl.multiple_of(step * CELLS, CELLS), CELLS), :]
    acc[...] += lax.dot_general(
        block, pair[...], (((0,), (0,)), ((), ())), preferred_element_type=F32
    )

    @pl.when(step == pl.num_programs(0) - 1)
    def _():
        scale = 1.0 / math.sqrt(float(NG**3))
        turned = (acc[...] * scale).T.reshape(128, 2, 8, 64)
        out[...] = jnp.concatenate([turned[:, 0], turned[:, 1]], axis=-1)


def project(got, pair, tab):
    steps = pair.shape[0] // CELLS
    whole = lambda shape: pl.BlockSpec(shape, lambda i: (0,) * len(shape))
    return pl.pallas_call(
        project_kernel,
        grid=(steps,),
        in_specs=[
            whole(got.shape),
            whole(tab["unswap"].shape),
            whole(tab["back"].shape),
            pl.BlockSpec((CELLS, pair.shape[1]), lambda i: (i, 0)),
        ],
        out_specs=whole((128, 8, 128)),
        out_shape=jax.ShapeDtypeStruct((128, 8, 128), F32),
        scratch_shapes=[
            pltpu.VMEM((MG * ROWS, 512), BF),
            pltpu.VMEM((pair.shape[0], 64), BF),
            pltpu.VMEM((64, pair.shape[1]), F32),
        ],
        compiler_params=pltpu.CompilerParams(vmem_limit_bytes=48 * 2**20),
        name="project",
    )(got, const(tab["unswap"]), const(tab["back"]), pair)


ROOM = 32
GROUP = 320


def parts_of(device):
    grid, vec = device // 8, device % 8
    return grid // 4, (vec // 4) * 2 + (grid // 2) % 2, grid % 2, vec % 4


def device_at(z, x, core, y):
    return (z * 4 + (x % 2) * 2 + core) * 8 + (x // 2) * 4 + y


def bring(data, dz=0, dx=0, dcore=0, dy=0):
    pairs = []
    for device in range(128):
        z, x, core, y = parts_of(device)
        source = device_at((z + dz) % 4, (x + dx) % 4, (core + dcore) % 2, (y + dy) % 4)
        pairs.append((source, device))
    return lax.ppermute(data, BOTH, pairs)


def place_kernel(count, slot, *refs):
    blocks, out, turned = refs[:count], refs[count], refs[count + 1]
    start = 0
    for block in blocks:
        rows = block.shape[0]
        turned[start : start + rows, :] = block[...]
        start += rows
    slots = turned.shape[0]
    chunk = 256
    for first in range(0, slot.shape[1], chunk):
        index = lax.broadcasted_iota(jnp.int32, (slots, chunk), 0)
        pick = jnp.where(index == slot[:, first : first + chunk], 1.0, 0.0).astype(BF)
        out[:, first : first + chunk] = lax.dot_general(
            turned[...], pick, (((0,), (0,)), ((), ())), preferred_element_type=F32
        ).astype(BF)


def place(slot, blocks):
    vmem = pl.BlockSpec(memory_space=pltpu.VMEM)
    norb = blocks[0].shape[1]
    slots = sum(block.shape[0] for block in blocks)
    return pl.pallas_call(
        functools.partial(place_kernel, len(blocks)),
        in_specs=[vmem] * (1 + len(blocks)),
        out_specs=vmem,
        out_shape=jax.ShapeDtypeStruct((norb, slot.shape[0]), BF),
        scratch_shapes=[pltpu.VMEM((slots, norb), BF)],
        compiler_params=pltpu.CompilerParams(vmem_limit_bytes=32 * 2**20),
        name="place",
    )(slot[None], *blocks)


def summed_rows(orbitals, points, me):
    row_count = orbitals.shape[0]
    local_pos = points - me * row_count
    inside = (local_pos >= 0) & (local_pos < row_count)
    picked = jnp.take(orbitals, jnp.clip(local_pos, 0, row_count - 1), axis=0)
    picked = jnp.where(inside[:, None], picked, jnp.zeros_like(picked)).astype(F32)
    return lax.psum(picked, BOTH).astype(BF).T


def ranks(label):
    index = lax.iota(jnp.int32, label.shape[0])
    same = (label[:, None] == label[None, :]) & (index[:, None] < index[None, :])
    return jnp.sum(same.astype(jnp.int32), axis=0)


def spread_rows(orbitals, points, me, owner, own_rank, group_rank):
    row_count = orbitals.shape[0]
    z, x, core, y = parts_of(owner)
    my_z, my_x, my_core, my_y = parts_of(me)
    room = lax.iota(jnp.int32, ROOM)
    mine = (owner == me)[None] & (own_rank[None] == room[:, None])
    pick = jnp.sum(jnp.where(mine, (points - me * row_count)[None], 0), axis=1)
    own = jnp.take(orbitals, pick, axis=0)
    line = jnp.concatenate([own] + [bring(own, dy=d) for d in (1, 2, 3)], axis=0)
    square = jnp.concatenate([line] + [bring(line, dz=d) for d in (1, 2, 3)], axis=0)
    spot = (z - my_z) % 4 * (4 * ROOM) + (y - my_y) % 4 * ROOM + own_rank
    group = lax.iota(jnp.int32, GROUP)
    here = ((x == my_x) & (core == my_core))[None] & (group_rank[None] == group[:, None])
    source = jnp.sum(jnp.where(here, spot[None] + 1, 0), axis=1) - 1
    choose = source[:, None] == lax.iota(jnp.int32, 16 * ROOM)[None]
    held = mm(choose.astype(BF), square).astype(BF)
    right, left = bring(held, dx=1), bring(held, dx=3)
    half = GROUP // 2
    far_a, far_b = bring(right[:half], dx=1), bring(left[half:], dx=3)
    blocks = [held, right, far_a, far_b, left]
    blocks = blocks + [bring(block, dcore=1) for block in blocks]
    slot = ((core - my_core) % 2 * 4 + (x - my_x) % 4) * GROUP + group_rank
    return place(slot, blocks)


def gather_rows(orbitals, points, me):
    owner = points // orbitals.shape[0]
    _, x, core, _ = parts_of(owner)
    own_rank, group_rank = ranks(owner), ranks(x * 2 + core)
    fits = (jnp.max(own_rank) < ROOM) & (jnp.max(group_rank) < GROUP)
    return lax.cond(
        fits,
        lambda: spread_rows(orbitals, points, me, owner, own_rank, group_rank),
        lambda: summed_rows(orbitals, points, me),
    )


def shards(orbitals, inverse_panel, points):
    tab = tables()
    vec_count = lax.axis_size("vec")
    devices = lax.axis_size("grid") * vec_count
    me = lax.axis_index("grid") * vec_count + lax.axis_index("vec")
    npoints, cols = inverse_panel.shape
    rows_t = gather_rows(orbitals, points, me)
    panel2 = jnp.concatenate([inverse_panel, inverse_panel], axis=1)
    pair, send = make_pairs(orbitals, rows_t, panel2, tab)
    planes = lax.all_to_all(send.reshape(devices, ROWS, 128), BOTH, 0, 0)
    first = (me // CG * MI).astype(jnp.int32).reshape(1)
    ret = solve(first, planes.reshape(devices * ROWS, 128), tab)
    got = lax.all_to_all(ret.reshape(devices, ROWS, 128), BOTH, 0, 0)
    parts = project(got.reshape(MG, CG, ROWS, 128), pair, tab)
    parts = lax.all_to_all(parts, BOTH, 0, 0)
    total = jnp.sum(parts, axis=0)
    return jnp.concatenate([total[:, :cols], total[:, cols:]], axis=0)


def solution(mesh):
    in_specs = (P(BOTH, None), P(), P())
    return jax.shard_map(
        shards, mesh=mesh, in_specs=in_specs, out_specs=P(BOTH, None), check_vma=False
    )
```

```python
import functools
import math

import jax
import jax.numpy as jnp
import numpy as np
from jax import lax
from jax.experimental import pallas as pl
from jax.experimental.pallas import tpu as pltpu
from jax.sharding import PartitionSpec as P

NG = 96
HALF = NG // 2
SCREEN = 2.25
AXES = ("z", "x_lo", "core", "x_hi", "y")
BF = jnp.bfloat16
F32 = jnp.float32

LINES = 72
OCT = LINES // 8
MG, MI = 32, 3
CG, CI = 4, 16
ROWS = 32
CELLS = 8 * NG
WIDE = 12 * NG


def basis_table():
    index = np.arange(NG)
    phase = (index[:, None] * index[None, :]) % NG
    angle = phase.astype(np.float32) * np.float32(2.0 * math.pi / NG)
    cos_tab = np.cos(angle).astype(BF).astype(np.float32)
    sin_tab = np.sin(angle).astype(BF).astype(np.float32)
    return np.concatenate([cos_tab[:, : HALF + 1], sin_tab[:, 1:HALF]], axis=1)


def tables():
    basis = basis_table()
    ahead = np.zeros((MG, ROWS, OCT, NG), np.float32)
    for octet in range(OCT):
        for mi in range(MI):
            ahead[:, octet * MI + mi, octet, :] = basis[:, mi::MI].T
    ahead = ahead.reshape(MG * ROWS, OCT * NG)
    lane = np.arange(512).reshape(8, CG, CI)
    order = lane.transpose(1, 0, 2).reshape(-1)
    swap = np.zeros((512, 512), np.float32)
    swap[order, np.arange(512)] = 1.0
    wide = np.kron(basis, np.eye(CI, dtype=np.float32))
    x_order = (3 * np.arange(32)[None, :] + np.arange(3)[:, None]).reshape(-1)
    x_basis = basis[x_order]
    return {
        "ahead": ahead,
        "back": ahead.T,
        "swap": swap,
        "unswap": swap.T,
        "wide": wide,
        "wide_t": wide.T,
        "x_ahead": x_basis.T,
        "x_back": x_basis,
    }


def const(array):
    return jnp.asarray(np.ascontiguousarray(array).astype(BF))


def mm(a, b):
    return jnp.dot(a, b, preferred_element_type=F32)


def pair_kernel(orb, rows_t, panel, ahead, swap, pair, send, fit):
    step = pl.program_id(0)
    npts = rows_t.shape[1]
    chunk = 256
    total = jnp.zeros((CELLS, 128), F32)
    for start in range(0, npts, chunk):
        corr = mm(orb[...], rows_t[:, start : start + chunk])
        block = (corr * corr).astype(BF)
        pair[:, start : start + chunk] = block
        total = total + mm(block, panel[start : start + chunk, :])
    low = lax.broadcasted_iota(jnp.int32, (NG, 128), 1) < 64
    for two in range(4):
        even = total[2 * two * NG : (2 * two + 1) * NG]
        odd = total[(2 * two + 1) * NG : (2 * two + 2) * NG]
        fit[pl.ds(pl.multiple_of(step * NG, NG), NG), two * 128 : (two + 1) * 128] = jnp.where(
            low, even, odd
        ).astype(BF)

    @pl.when(step == pl.num_programs(0) - 1)
    def _():
        for part in range(4):
            rows = MG * ROWS // 4
            spec = mm(ahead[part * rows : (part + 1) * rows, :], fit[...]).astype(BF)
            moved = mm(spec, swap[...]).astype(BF)
            for cg in range(CG):
                send[part * MG // 4 : (part + 1) * MG // 4, cg] = moved[
                    :, cg * 128 : (cg + 1) * 128
                ].reshape(MG // 4, ROWS, 128)


def make_pairs(orbitals, rows_t, panel2, tab):
    npts = rows_t.shape[1]
    norb = orbitals.shape[1]
    steps = orbitals.shape[0] // CELLS
    whole = lambda shape: pl.BlockSpec(shape, lambda i: (0,) * len(shape))
    return pl.pallas_call(
        pair_kernel,
        grid=(steps,),
        in_specs=[
            pl.BlockSpec((CELLS, norb), lambda i: (i, 0)),
            whole(rows_t.shape),
            whole(panel2.shape),
            whole(tab["ahead"].shape),
            whole(tab["swap"].shape),
        ],
        out_specs=[
            pl.BlockSpec((CELLS, npts), lambda i: (i, 0)),
            whole((MG, CG, ROWS, 128)),
        ],
        out_shape=[
            jax.ShapeDtypeStruct((orbitals.shape[0], npts), BF),
            jax.ShapeDtypeStruct((MG, CG, ROWS, 128), BF),
        ],
        scratch_shapes=[pltpu.VMEM((OCT * NG, 512), BF)],
        compiler_params=pltpu.CompilerParams(vmem_limit_bytes=48 * 2**20),
        name="pairs",
    )(orbitals, rows_t, panel2, const(tab["ahead"]), const(tab["swap"]))


def places():
    for part in range(4):
        for octet in range(OCT):
            for mi in range(MI):
                spot = part * OCT + octet
                yield part * ROWS + octet * MI + mi, mi, spot // 12, spot % 12


def solve_kernel(first, got, wide, wide_t, x_ahead, x_back, out, flat, field):
    flat[...] = got[...].astype(F32)
    for row, mi, xr, yo in places():
        field[mi, xr * 32 : (xr + 1) * 32, yo * 128 : (yo + 1) * 128] = flat[
            pl.ds(row, 32, stride=4 * ROWS), :
        ].astype(BF)
    lane = lax.broadcasted_iota(jnp.int32, (1, NG * CI), 1) // CI
    subl = lax.broadcasted_iota(jnp.int32, (NG, 1), 0)
    wave_of = lambda k: jnp.where(k <= HALF, k, k - HALF)
    weight = lambda w: jnp.where((w == 0) | (w == HALF), 1.0, 2.0).astype(F32)
    wave_y, wave_x = wave_of(lane), wave_of(subl)
    square = lambda w: w.astype(F32) * w.astype(F32)
    factor = NG / (2.0 * math.pi) * (NG / (2.0 * math.pi))
    flat[...] = jnp.zeros_like(flat)
    spec_y = mm(field[...].reshape(MI * NG, NG * CI), wide[...]).astype(BF)
    backs = []
    for mi in range(MI):
        wave_z = wave_of(first[0] + mi)
        spec = mm(x_ahead[...], spec_y[mi * NG : (mi + 1) * NG])
        total = square(wave_x) + square(wave_y) + square(wave_z)
        gain = weight(wave_x) * (weight(wave_y) * weight(wave_z))
        kernel = jnp.where(total > 0.5, factor / (total + SCREEN), 0.0) * gain
        scaled = (spec * kernel).astype(BF)
        backs.append(mm(x_back[...], scaled).astype(BF))
    plane = mm(jnp.concatenate(backs, axis=0), wide_t[...])
    for row, mi, xr, yo in places():
        flat[pl.ds(row, 32, stride=4 * ROWS), :] = plane[
            mi * NG + xr * 32 : mi * NG + (xr + 1) * 32, yo * 128 : (yo + 1) * 128
        ]
    out[...] = flat[...].astype(BF)


def solve(first, got, tab):
    vmem = pl.BlockSpec(memory_space=pltpu.VMEM)
    return pl.pallas_call(
        solve_kernel,
        in_specs=[pl.BlockSpec(memory_space=pltpu.SMEM)] + [vmem] * 5,
        out_specs=vmem,
        out_shape=jax.ShapeDtypeStruct(got.shape, BF),
        scratch_shapes=[
            pltpu.VMEM(got.shape, F32),
            pltpu.VMEM((MI, NG, NG * CI), BF),
        ],
        compiler_params=pltpu.CompilerParams(vmem_limit_bytes=48 * 2**20),
        name="solve",
    )(
        first,
        got,
        const(tab["wide"]),
        const(tab["wide_t"]),
        const(tab["x_ahead"]),
        const(tab["x_back"]),
    )


def project_kernel(got, unswap, back, pair, out, spec, pot, acc):
    step = pl.program_id(0)

    @pl.when(step == 0)
    def _():
        for part in range(4):
            rows = MG * ROWS // 4
            block = jnp.concatenate(
                [
                    got[part * MG // 4 : (part + 1) * MG // 4, cg].reshape(rows, 128)
                    for cg in range(CG)
                ],
                axis=1,
            )
            spec[part * rows : (part + 1) * rows, :] = mm(block, unswap[...]).astype(BF)
        for octet in range(OCT):
            final = mm(back[octet * NG : (octet + 1) * NG, :], spec[...])
            final = final / float(NG**3)
            for yi in range(8):
                start = (octet * 8 + yi) * NG
                pot[start : start + NG, :] = final[:, yi * 64 : (yi + 1) * 64].astype(BF)
        acc[...] = jnp.zeros_like(acc)

    block = pot[pl.ds(pl.multiple_of(step * WIDE, WIDE), WIDE), :]
    acc[...] += lax.dot_general(
        block, pair[...], (((0,), (0,)), ((), ())), preferred_element_type=F32
    )

    @pl.when(step == pl.num_programs(0) - 1)
    def _():
        scale = 1.0 / math.sqrt(float(NG**3))
        turned = (acc[...] * scale).T.reshape(128, 2, 8, 64)
        out[...] = jnp.concatenate([turned[:, 0], turned[:, 1]], axis=-1)


def project(got, pair, tab):
    steps = pair.shape[0] // WIDE
    whole = lambda shape: pl.BlockSpec(shape, lambda i: (0,) * len(shape))
    return pl.pallas_call(
        project_kernel,
        grid=(steps,),
        in_specs=[
            whole(got.shape),
            whole(tab["unswap"].shape),
            whole(tab["back"].shape),
            pl.BlockSpec((WIDE, pair.shape[1]), lambda i: (i, 0)),
        ],
        out_specs=whole((128, 8, 128)),
        out_shape=jax.ShapeDtypeStruct((128, 8, 128), F32),
        scratch_shapes=[
            pltpu.VMEM((MG * ROWS, 512), BF),
            pltpu.VMEM((pair.shape[0], 64), BF),
            pltpu.VMEM((64, pair.shape[1]), F32),
        ],
        compiler_params=pltpu.CompilerParams(vmem_limit_bytes=48 * 2**20),
        name="project",
    )(got, const(tab["unswap"]), const(tab["back"]), pair)


ROOM = 32
GROUP = 320


def parts_of(device):
    grid, vec = device // 8, device % 8
    return grid // 4, (vec // 4) * 2 + (grid // 2) % 2, grid % 2, vec % 4


def device_at(z, x, core, y):
    return (z * 4 + (x % 2) * 2 + core) * 8 + (x // 2) * 4 + y


def bring(data, dz=0, dx=0, dcore=0, dy=0):
    pairs = []
    for device in range(128):
        z, x, core, y = parts_of(device)
        source = device_at((z + dz) % 4, (x + dx) % 4, (core + dcore) % 2, (y + dy) % 4)
        pairs.append((source, device))
    return lax.ppermute(data, AXES, pairs)


def place_kernel(count, slot, *refs):
    blocks, out, turned = refs[:count], refs[count], refs[count + 1]
    start = 0
    for block in blocks:
        rows = block.shape[0]
        turned[start : start + rows, :] = block[...]
        start += rows
    slots = turned.shape[0]
    chunk = 256
    for first in range(0, slot.shape[1], chunk):
        index = lax.broadcasted_iota(jnp.int32, (slots, chunk), 0)
        pick = jnp.where(index == slot[:, first : first + chunk], 1.0, 0.0).astype(BF)
        out[:, first : first + chunk] = lax.dot_general(
            turned[...], pick, (((0,), (0,)), ((), ())), preferred_element_type=F32
        ).astype(BF)


def place(slot, blocks):
    vmem = pl.BlockSpec(memory_space=pltpu.VMEM)
    norb = blocks[0].shape[1]
    slots = sum(block.shape[0] for block in blocks)
    return pl.pallas_call(
        functools.partial(place_kernel, len(blocks)),
        in_specs=[vmem] * (1 + len(blocks)),
        out_specs=vmem,
        out_shape=jax.ShapeDtypeStruct((norb, slot.shape[1]), BF),
        scratch_shapes=[pltpu.VMEM((slots, norb), BF)],
        compiler_params=pltpu.CompilerParams(vmem_limit_bytes=32 * 2**20),
        name="place",
    )(slot, *blocks)


def summed_rows(orbitals, points, me):
    row_count = orbitals.shape[0]
    local_pos = points - me * row_count
    inside = (local_pos >= 0) & (local_pos < row_count)
    picked = jnp.take(orbitals, jnp.clip(local_pos, 0, row_count - 1), axis=0)
    picked = jnp.where(inside[:, None], picked, jnp.zeros_like(picked)).astype(F32)
    return lax.psum(picked, AXES).astype(BF).T


def index_kernel(me, points, orbitals, fits, own, choose, slot, picks, spots, near, sems, one):
    npts = points.shape[1]
    row_count = orbitals.shape[0]
    my_z, my_x, my_core, my_y = parts_of(me[0])
    owner = ((points[...].astype(F32) + 0.5) * (1.0 / row_count)).astype(jnp.int32)
    z, y, core = owner >> 5, owner & 3, (owner >> 3) & 1
    x = ((owner >> 2) & 1) * 2 + ((owner >> 4) & 1)
    group = x * 2 + core
    size = 256
    early = lax.broadcasted_iota(jnp.int32, (size, size), 0) < lax.broadcasted_iota(
        jnp.int32, (size, size), 1
    )
    early = jnp.where(early, 1.0, 0.0).astype(BF)

    def ranks(label, labels):
        index = lax.broadcasted_iota(jnp.int32, (labels, size), 0)
        seen = jnp.zeros((labels, 1), F32)
        found = []
        for first in range(0, npts, size):
            match = jnp.where(index == label[:, first : first + size], 1.0, 0.0)
            before = mm(match.astype(BF), early) + seen
            found.append(jnp.sum(match * before, axis=0, keepdims=True))
            seen = seen + jnp.sum(match, axis=1, keepdims=True)
        return jnp.concatenate(found, axis=1).astype(jnp.int32), jnp.max(seen)

    own_rank, own_most = ranks(owner, 128)
    group_rank, group_most = ranks(group, 16)
    fits[0] = ((own_most <= ROOM) & (group_most <= GROUP)).astype(jnp.int32)

    def lookup(key, value, first, rows):
        number = lax.broadcasted_iota(jnp.int32, (rows, 128), 0) + first
        total = jnp.zeros((rows, 128), jnp.int32)
        for start in range(0, npts, 128):
            total = total + jnp.where(
                key[:, start : start + 128] == number, value[:, start : start + 128], 0
            )
        return jnp.sum(total.astype(F32), axis=1, keepdims=True).astype(jnp.int32)

    key = jnp.where(owner == me[0], own_rank, -1)
    pick = lookup(key, points[...] - me[0] * row_count, 0, ROOM)
    picks[...] = jnp.broadcast_to(pick, (ROOM, 128))
    move = pltpu.make_async_copy(picks, spots, one)
    move.start()
    move.wait()
    copies = []
    for place in range(ROOM):
        start = pl.multiple_of((spots[place, 0] >> 4) << 4, 16)
        copies.append(
            pltpu.make_async_copy(
                orbitals.at[pl.ds(start, 16), :],
                near.at[pl.ds(place * 16, 16), :],
                sems.at[place],
            )
        )
        copies[-1].start()

    spot = z * (4 * ROOM) + y * ROOM + own_rank
    key = jnp.where((x == my_x) & (core == my_core), group_rank, -1)
    for first in range(0, GROUP, 64):
        source = lookup(key, spot + 1, first, 64) - 1
        lane = lax.broadcasted_iota(jnp.int32, (64, 16 * ROOM), 1)
        choose[first : first + 64, :] = jnp.where(source == lane, 1.0, 0.0).astype(BF)
    slot[...] = (((core - my_core) & 1) * 4 + ((x - my_x) & 3)) * GROUP + group_rank
    for copy in copies:
        copy.wait()
    lane = lax.broadcasted_iota(jnp.int32, (ROOM, 16 * ROOM), 1)
    line = lax.broadcasted_iota(jnp.int32, (ROOM, 16 * ROOM), 0)
    select = jnp.where(lane == line * 16 + (pick & 15), 1.0, 0.0).astype(BF)
    own[...] = mm(select, near[...]).astype(BF)


def index(me, points, orbitals):
    vmem = pl.BlockSpec(memory_space=pltpu.VMEM)
    smem = pl.BlockSpec(memory_space=pltpu.SMEM)
    npts, norb = points.shape[0], orbitals.shape[1]
    return pl.pallas_call(
        index_kernel,
        in_specs=[smem, vmem, pl.BlockSpec(memory_space=pl.ANY)],
        out_specs=[smem, vmem, vmem, vmem],
        out_shape=[
            jax.ShapeDtypeStruct((1,), jnp.int32),
            jax.ShapeDtypeStruct((ROOM, norb), BF),
            jax.ShapeDtypeStruct((GROUP, 16 * ROOM), BF),
            jax.ShapeDtypeStruct((1, npts), jnp.int32),
        ],
        scratch_shapes=[
            pltpu.VMEM((ROOM, 128), jnp.int32),
            pltpu.SMEM((ROOM, 128), jnp.int32),
            pltpu.VMEM((16 * ROOM, norb), BF),
            pltpu.SemaphoreType.DMA((ROOM,)),
            pltpu.SemaphoreType.DMA,
        ],
        compiler_params=pltpu.CompilerParams(vmem_limit_bytes=16 * 2**20),
        name="index",
    )(me.reshape(1), points[None], orbitals)


def gather_rows(orbitals, points, me):
    fits, own, choose, slot = index(me, points, orbitals)
    copies = jnp.broadcast_to(own[None], (16,) + own.shape)
    square = lax.all_to_all(copies, ("z", "y"), 0, 0).reshape(16 * ROOM, own.shape[1])
    held = mm(choose, square).astype(BF)
    right, left = bring(held, dx=1), bring(held, dx=3)
    half = GROUP // 2
    far_a, far_b = bring(right[:half], dx=1), bring(left[half:], dx=3)
    blocks = [held, right, far_a, far_b, left]
    blocks = blocks + [bring(block, dcore=1) for block in blocks]
    return lax.cond(
        fits[0] > 0,
        lambda: place(slot, blocks),
        lambda: summed_rows(orbitals, points, me),
    )


def shards(orbitals, inverse_panel, points):
    tab = tables()
    devices = lax.axis_size(AXES)
    me = lax.axis_index(AXES)
    npoints, cols = inverse_panel.shape
    rows_t = gather_rows(orbitals, points, me)
    panel2 = jnp.concatenate([inverse_panel, inverse_panel], axis=1)
    pair, send = make_pairs(orbitals, rows_t, panel2, tab)
    planes = lax.all_to_all(send.reshape(devices, ROWS, 128), AXES, 0, 0)
    first = (me // CG * MI).astype(jnp.int32).reshape(1)
    ret = solve(first, planes.reshape(devices * ROWS, 128), tab)
    got = lax.all_to_all(ret.reshape(devices, ROWS, 128), AXES, 0, 0)
    parts = project(got.reshape(MG, CG, ROWS, 128), pair, tab)
    parts = lax.all_to_all(parts, AXES, 0, 0)
    total = jnp.sum(parts, axis=0)
    return jnp.concatenate([total[:, :cols], total[:, cols:]], axis=0)


def solution(mesh):
    fine = jax.sharding.Mesh(mesh.devices.reshape(4, 2, 2, 2, 4), AXES)
    in_specs = (P(AXES, None), P(), P())
    return jax.shard_map(
        shards, mesh=fine, in_specs=in_specs, out_specs=P(AXES, None), check_vma=False
    )
```

```python
import functools
import math

import jax
import jax.numpy as jnp
import numpy as np
from jax import lax
from jax.experimental import pallas as pl
from jax.experimental.pallas import tpu as pltpu
from jax.sharding import PartitionSpec as P

NG = 96
HALF = NG // 2
SCREEN = 2.25
AXES = ("z", "x_lo", "core", "x_hi", "y")
BF = jnp.bfloat16
F32 = jnp.float32

LINES = 72
OCT = LINES // 8
MG, MI = 32, 3
CG, CI = 4, 16
ROWS = 32
CELLS = 8 * NG
WIDE = 9 * NG


def basis_table():
    index = np.arange(NG)
    phase = (index[:, None] * index[None, :]) % NG
    angle = phase.astype(np.float32) * np.float32(2.0 * math.pi / NG)
    cos_tab = np.cos(angle).astype(BF).astype(np.float32)
    sin_tab = np.sin(angle).astype(BF).astype(np.float32)
    return np.concatenate([cos_tab[:, : HALF + 1], sin_tab[:, 1:HALF]], axis=1)


def tables():
    basis = basis_table()
    ahead = np.zeros((MG, ROWS, OCT, NG), np.float32)
    for octet in range(OCT):
        for mi in range(MI):
            ahead[:, octet * MI + mi, octet, :] = basis[:, mi::MI].T
    ahead = ahead.reshape(MG * ROWS, OCT * NG)
    lane = np.arange(512).reshape(8, CG, CI)
    order = lane.transpose(1, 0, 2).reshape(-1)
    swap = np.zeros((512, 512), np.float32)
    swap[order, np.arange(512)] = 1.0
    wide = np.kron(basis, np.eye(CI, dtype=np.float32))
    x_order = (3 * np.arange(32)[None, :] + np.arange(3)[:, None]).reshape(-1)
    x_basis = basis[x_order]
    return {
        "ahead": ahead,
        "back": ahead.T,
        "swap": swap,
        "unswap": swap.T,
        "wide": wide,
        "x_ahead": x_basis.T,
        "x_back": x_basis,
    }


def const(array):
    return jnp.asarray(np.ascontiguousarray(array).astype(BF))


def mm(a, b):
    return jnp.dot(a, b, preferred_element_type=F32)


def pair_kernel(orb, rows_t, panel, ahead, swap, pair, send, fit):
    step = pl.program_id(0)
    npts = rows_t.shape[1]
    chunk = 256
    total = jnp.zeros((CELLS, 128), F32)
    for start in range(0, npts, chunk):
        corr = mm(orb[...], rows_t[:, start : start + chunk])
        block = (corr * corr).astype(BF)
        pair[:, start : start + chunk] = block
        total = total + mm(block, panel[start : start + chunk, :])
    low = lax.broadcasted_iota(jnp.int32, (NG, 128), 1) < 64
    for two in range(4):
        even = total[2 * two * NG : (2 * two + 1) * NG]
        odd = total[(2 * two + 1) * NG : (2 * two + 2) * NG]
        fit[pl.ds(pl.multiple_of(step * NG, NG), NG), two * 128 : (two + 1) * 128] = jnp.where(
            low, even, odd
        ).astype(BF)

    @pl.when(step == pl.num_programs(0) - 1)
    def _():
        for part in range(4):
            rows = MG * ROWS // 4
            spec = mm(ahead[part * rows : (part + 1) * rows, :], fit[...]).astype(BF)
            moved = mm(spec, swap[...]).astype(BF)
            for cg in range(CG):
                send[part * MG // 4 : (part + 1) * MG // 4, cg] = moved[
                    :, cg * 128 : (cg + 1) * 128
                ].reshape(MG // 4, ROWS, 128)


def make_pairs(orbitals, rows_t, panel2, tab):
    npts = rows_t.shape[1]
    norb = orbitals.shape[1]
    steps = orbitals.shape[0] // CELLS
    whole = lambda shape: pl.BlockSpec(shape, lambda i: (0,) * len(shape))
    return pl.pallas_call(
        pair_kernel,
        grid=(steps,),
        in_specs=[
            pl.BlockSpec((CELLS, norb), lambda i: (i, 0)),
            whole(rows_t.shape),
            whole(panel2.shape),
            whole(tab["ahead"].shape),
            whole(tab["swap"].shape),
        ],
        out_specs=[
            pl.BlockSpec((CELLS, npts), lambda i: (i, 0)),
            whole((MG, CG, ROWS, 128)),
        ],
        out_shape=[
            jax.ShapeDtypeStruct((orbitals.shape[0], npts), BF),
            jax.ShapeDtypeStruct((MG, CG, ROWS, 128), BF),
        ],
        scratch_shapes=[pltpu.VMEM((OCT * NG, 512), BF)],
        compiler_params=pltpu.CompilerParams(vmem_limit_bytes=28 * 2**20),
        name="pairs",
    )(orbitals, rows_t, panel2, const(tab["ahead"]), const(tab["swap"]))


def places():
    for part in range(4):
        for octet in range(OCT):
            for mi in range(MI):
                spot = part * OCT + octet
                yield part * ROWS + octet * MI + mi, mi, spot // 12, spot % 12


def solve_kernel(first, got, table, x_ahead, x_back, out, flat, field, wide, sem):
    fetch = pltpu.make_async_copy(table, wide, sem)
    fetch.start()
    flat[...] = got[...].astype(F32)
    for row, mi, xr, yo in places():
        field[mi, xr * 32 : (xr + 1) * 32, yo * 128 : (yo + 1) * 128] = flat[
            pl.ds(row, 32, stride=4 * ROWS), :
        ].astype(BF)
    lane = lax.broadcasted_iota(jnp.int32, (1, NG * CI), 1) // CI
    subl = lax.broadcasted_iota(jnp.int32, (NG, 1), 0)
    wave_of = lambda k: jnp.where(k <= HALF, k, k - HALF)
    weight = lambda w: jnp.where((w == 0) | (w == HALF), 1.0, 2.0).astype(F32)
    wave_y, wave_x = wave_of(lane), wave_of(subl)
    square = lambda w: w.astype(F32) * w.astype(F32)
    factor = NG / (2.0 * math.pi) * (NG / (2.0 * math.pi))
    flat[...] = jnp.zeros_like(flat)
    fetch.wait()
    spec_y = mm(field[...].reshape(MI * NG, NG * CI), wide[...]).astype(BF)
    backs = []
    for mi in range(MI):
        wave_z = wave_of(first[0] + mi)
        spec = mm(x_ahead[...], spec_y[mi * NG : (mi + 1) * NG])
        total = square(wave_x) + square(wave_y) + square(wave_z)
        gain = weight(wave_x) * (weight(wave_y) * weight(wave_z))
        kernel = jnp.where(total > 0.5, factor / (total + SCREEN), 0.0) * gain
        scaled = (spec * kernel).astype(BF)
        backs.append(mm(x_back[...], scaled).astype(BF))
    plane = lax.dot_general(
        jnp.concatenate(backs, axis=0),
        wide[...],
        (((1,), (1,)), ((), ())),
        preferred_element_type=F32,
    )
    for row, mi, xr, yo in places():
        flat[pl.ds(row, 32, stride=4 * ROWS), :] = plane[
            mi * NG + xr * 32 : mi * NG + (xr + 1) * 32, yo * 128 : (yo + 1) * 128
        ]
    out[...] = flat[...].astype(BF)


def solve(first, got, tab):
    vmem = pl.BlockSpec(memory_space=pltpu.VMEM)
    return pl.pallas_call(
        solve_kernel,
        in_specs=[pl.BlockSpec(memory_space=pltpu.SMEM), vmem, pl.BlockSpec(memory_space=pl.ANY)]
        + [vmem] * 2,
        out_specs=vmem,
        out_shape=jax.ShapeDtypeStruct(got.shape, BF),
        scratch_shapes=[
            pltpu.VMEM(got.shape, F32),
            pltpu.VMEM((MI, NG, NG * CI), BF),
            pltpu.VMEM(tab["wide"].shape, BF),
            pltpu.SemaphoreType.DMA,
        ],
        compiler_params=pltpu.CompilerParams(vmem_limit_bytes=48 * 2**20),
        name="solve",
    )(
        first,
        got,
        const(tab["wide"]),
        const(tab["x_ahead"]),
        const(tab["x_back"]),
    )


def project_kernel(got, unswap, back, pair, out, spec, pot, acc, near, sems):
    steps = pair.shape[0] // WIDE
    blocks = [pl.ds(step * WIDE, WIDE) for step in range(steps)]
    copies = [
        pltpu.make_async_copy(pair.at[rows, :], near.at[rows, :], sems.at[step])
        for step, rows in enumerate(blocks)
    ]
    for copy in copies:
        copy.start()
    for part in range(4):
        rows = MG * ROWS // 4
        block = jnp.concatenate(
            [
                got[part * MG // 4 : (part + 1) * MG // 4, cg].reshape(rows, 128)
                for cg in range(CG)
            ],
            axis=1,
        )
        spec[part * rows : (part + 1) * rows, :] = mm(block, unswap[...]).astype(BF)
    for octet in range(OCT):
        final = mm(back[octet * NG : (octet + 1) * NG, :], spec[...])
        final = final / float(NG**3)
        for yi in range(8):
            start = (octet * 8 + yi) * NG
            pot[start : start + NG, :] = final[:, yi * 64 : (yi + 1) * 64].astype(BF)
    acc[...] = jnp.zeros_like(acc)
    for copy, rows in zip(copies, blocks):
        copy.wait()
        acc[...] += lax.dot_general(
            pot[rows, :], near[rows, :], (((0,), (0,)), ((), ())), preferred_element_type=F32
        )
    scale = 1.0 / math.sqrt(float(NG**3))
    turned = (acc[...] * scale).T.reshape(128, 2, 8, 64)
    out[...] = jnp.concatenate([turned[:, 0], turned[:, 1]], axis=-1)


def project(got, pair, tab):
    vmem = pl.BlockSpec(memory_space=pltpu.VMEM)
    return pl.pallas_call(
        project_kernel,
        in_specs=[vmem] * 3 + [pl.BlockSpec(memory_space=pl.ANY)],
        out_specs=vmem,
        out_shape=jax.ShapeDtypeStruct((128, 8, 128), F32),
        scratch_shapes=[
            pltpu.VMEM((MG * ROWS, 512), BF),
            pltpu.VMEM((pair.shape[0], 64), BF),
            pltpu.VMEM((64, pair.shape[1]), F32),
            pltpu.VMEM(pair.shape, BF),
            pltpu.SemaphoreType.DMA((pair.shape[0] // WIDE,)),
        ],
        compiler_params=pltpu.CompilerParams(vmem_limit_bytes=44 * 2**20),
        name="project",
    )(got, const(tab["unswap"]), const(tab["back"]), pair)


ROOM = 32
GROUP = 320


def parts_of(device):
    grid, vec = device // 8, device % 8
    return grid // 4, (vec // 4) * 2 + (grid // 2) % 2, grid % 2, vec % 4


def device_at(z, x, core, y):
    return (z * 4 + (x % 2) * 2 + core) * 8 + (x // 2) * 4 + y


def bring(data, dz=0, dx=0, dcore=0, dy=0):
    pairs = []
    for device in range(128):
        z, x, core, y = parts_of(device)
        source = device_at((z + dz) % 4, (x + dx) % 4, (core + dcore) % 2, (y + dy) % 4)
        pairs.append((source, device))
    return lax.ppermute(data, AXES, pairs)


def place_kernel(count, base, *refs):
    blocks, (slot, *more), (out, held) = refs[:count], refs[count:-2], refs[-2:]
    start = 0
    for block in blocks:
        rows = block.shape[0]
        held[start : start + rows, :] = block[...]
        start += rows
    chunk = 256
    for first in range(0, slot.shape[1], chunk):
        wanted = slot[:, first : first + chunk]
        picks = []
        for block, number in zip(blocks, base):
            index = lax.broadcasted_iota(jnp.int32, (block.shape[0], chunk), 0) + number
            picks.append(jnp.where(index == wanted, 1.0, 0.0).astype(BF))
        total = lax.dot_general(
            held[...],
            jnp.concatenate(picks, axis=0),
            (((0,), (0,)), ((), ())),
            preferred_element_type=F32,
        )
        if more:
            total = total + more[0][:, first : first + chunk].astype(F32)
        out[:, first : first + chunk] = total.astype(BF)


def place(slot, blocks, base, more=()):
    vmem = pl.BlockSpec(memory_space=pltpu.VMEM)
    norb, npts = blocks[0].shape[1], slot.shape[1]
    slots = sum(block.shape[0] for block in blocks)
    return pl.pallas_call(
        functools.partial(place_kernel, len(blocks), base),
        in_specs=[vmem] * (1 + len(blocks) + len(more)),
        out_specs=vmem,
        out_shape=jax.ShapeDtypeStruct((norb, npts), BF),
        scratch_shapes=[pltpu.VMEM((slots, norb), BF)],
        compiler_params=pltpu.CompilerParams(vmem_limit_bytes=20 * 2**20),
        cost_estimate=pl.CostEstimate(
            flops=2 * slots * norb * npts, bytes_accessed=4 * norb * npts, transcendentals=0
        ),
        name="place",
    )(*blocks, slot, *more)


def summed_rows(orbitals, points, me):
    row_count = orbitals.shape[0]
    local_pos = points - me * row_count
    inside = (local_pos >= 0) & (local_pos < row_count)
    picked = jnp.take(orbitals, jnp.clip(local_pos, 0, row_count - 1), axis=0)
    picked = jnp.where(inside[:, None], picked, jnp.zeros_like(picked)).astype(F32)
    return lax.psum(picked, AXES).astype(BF).T


def index_kernel(me, points, orbitals, fits, own, choose, slot, picks, spots, near, sems, one):
    npts = points.shape[1]
    row_count = orbitals.shape[0]
    my_z, my_x, my_core, my_y = parts_of(me[0])
    owner = ((points[...].astype(F32) + 0.5) * (1.0 / row_count)).astype(jnp.int32)
    z, y, core = owner >> 5, owner & 3, (owner >> 3) & 1
    x = ((owner >> 2) & 1) * 2 + ((owner >> 4) & 1)
    group = x * 2 + core
    size = 256
    early = lax.broadcasted_iota(jnp.int32, (size, size), 0) < lax.broadcasted_iota(
        jnp.int32, (size, size), 1
    )
    early = jnp.where(early, 1.0, 0.0).astype(BF)

    def ranks(label, labels):
        index = lax.broadcasted_iota(jnp.int32, (labels, size), 0)
        seen = jnp.zeros((labels, 1), F32)
        found = []
        for first in range(0, npts, size):
            match = jnp.where(index == label[:, first : first + size], 1.0, 0.0)
            before = mm(match.astype(BF), early) + seen
            found.append(jnp.sum(match * before, axis=0, keepdims=True))
            seen = seen + jnp.sum(match, axis=1, keepdims=True)
        return jnp.concatenate(found, axis=1).astype(jnp.int32), jnp.max(seen)

    own_rank, own_most = ranks(owner, 128)
    group_rank, group_most = ranks(group, 16)
    fits[0] = ((own_most <= ROOM) & (group_most <= GROUP)).astype(jnp.int32)

    def lookup(key, value, first, rows):
        number = lax.broadcasted_iota(jnp.int32, (rows, 128), 0) + first
        total = jnp.zeros((rows, 128), jnp.int32)
        for start in range(0, npts, 128):
            total = total + jnp.where(
                key[:, start : start + 128] == number, value[:, start : start + 128], 0
            )
        return jnp.sum(total.astype(F32), axis=1, keepdims=True).astype(jnp.int32)

    key = jnp.where(owner == me[0], own_rank, -1)
    pick = lookup(key, points[...] - me[0] * row_count, 0, ROOM)
    picks[...] = jnp.broadcast_to(pick, (ROOM, 128))
    move = pltpu.make_async_copy(picks, spots, one)
    move.start()
    move.wait()
    copies = []
    for place in range(ROOM):
        start = pl.multiple_of((spots[place, 0] >> 4) << 4, 16)
        copies.append(
            pltpu.make_async_copy(
                orbitals.at[pl.ds(start, 16), :],
                near.at[pl.ds(place * 16, 16), :],
                sems.at[place],
            )
        )
        copies[-1].start()

    spot = z * (4 * ROOM) + y * ROOM + own_rank
    key = jnp.where((x == my_x) & (core == my_core), group_rank, -1)
    for first in range(0, GROUP, 64):
        source = lookup(key, spot + 1, first, 64) - 1
        lane = lax.broadcasted_iota(jnp.int32, (64, 16 * ROOM), 1)
        choose[first : first + 64, :] = jnp.where(source == lane, 1.0, 0.0).astype(BF)
    slot[...] = (((core - my_core) & 1) * 4 + ((x - my_x) & 3)) * GROUP + group_rank
    for copy in copies:
        copy.wait()
    lane = lax.broadcasted_iota(jnp.int32, (ROOM, 16 * ROOM), 1)
    line = lax.broadcasted_iota(jnp.int32, (ROOM, 16 * ROOM), 0)
    select = jnp.where(lane == line * 16 + (pick & 15), 1.0, 0.0).astype(BF)
    own[...] = mm(select, near[...]).astype(BF)


def index(me, points, orbitals):
    vmem = pl.BlockSpec(memory_space=pltpu.VMEM)
    smem = pl.BlockSpec(memory_space=pltpu.SMEM)
    npts, norb = points.shape[0], orbitals.shape[1]
    return pl.pallas_call(
        index_kernel,
        in_specs=[smem, vmem, pl.BlockSpec(memory_space=pl.ANY)],
        out_specs=[smem, vmem, vmem, vmem],
        out_shape=[
            jax.ShapeDtypeStruct((1,), jnp.int32),
            jax.ShapeDtypeStruct((ROOM, norb), BF),
            jax.ShapeDtypeStruct((GROUP, 16 * ROOM), BF),
            jax.ShapeDtypeStruct((1, npts), jnp.int32),
        ],
        scratch_shapes=[
            pltpu.VMEM((ROOM, 128), jnp.int32),
            pltpu.SMEM((ROOM, 128), jnp.int32),
            pltpu.VMEM((16 * ROOM, norb), BF),
            pltpu.SemaphoreType.DMA((ROOM,)),
            pltpu.SemaphoreType.DMA,
        ],
        compiler_params=pltpu.CompilerParams(vmem_limit_bytes=16 * 2**20),
        name="index",
    )(me.reshape(1), points[None], orbitals)


def spread_rows(own, choose, slot):
    copies = jnp.broadcast_to(own[None], (16,) + own.shape)
    square = lax.all_to_all(copies, ("z", "y"), 0, 0).reshape(16 * ROOM, own.shape[1])
    held = mm(choose, square).astype(BF)
    mate = lambda block: bring(block, dcore=1)
    half, ring = GROUP // 2, 4 * GROUP
    right, left = bring(held, dx=1), bring(held, dx=3)
    rows = place(slot, [held, mate(held)], (0, ring))
    far_a, far_b = bring(right[:half], dx=1), bring(left[half:], dx=3)
    near = [right, left, mate(right), mate(left)]
    rows = place(slot, near, (GROUP, 3 * GROUP, ring + GROUP, ring + 3 * GROUP), (rows,))
    far_a, far_b, rows = lax.optimization_barrier((far_a, far_b, rows))
    far = [far_a, far_b, mate(far_a), mate(far_b)]
    start = 2 * GROUP
    return place(slot, far, (start, start + half, ring + start, ring + start + half), (rows,))


def gather_rows(orbitals, points, me):
    fits, own, choose, slot = index(me, points, orbitals)
    return lax.cond(
        fits[0] > 0,
        lambda: spread_rows(own, choose, slot),
        lambda: summed_rows(orbitals, points, me),
    )


def shards(orbitals, inverse_panel, points):
    tab = tables()
    devices = lax.axis_size(AXES)
    me = lax.axis_index(AXES)
    npoints, cols = inverse_panel.shape
    rows_t = gather_rows(orbitals, points, me)
    panel2 = jnp.concatenate([inverse_panel, inverse_panel], axis=1)
    pair, send = make_pairs(orbitals, rows_t, panel2, tab)
    planes = lax.all_to_all(send.reshape(devices, ROWS, 128), AXES, 0, 0)
    first = (me // CG * MI).astype(jnp.int32).reshape(1)
    ret = solve(first, planes.reshape(devices * ROWS, 128), tab)
    got = lax.all_to_all(ret.reshape(devices, ROWS, 128), AXES, 0, 0)
    parts = project(got.reshape(MG, CG, ROWS, 128), pair, tab)
    parts = lax.all_to_all(parts, AXES, 0, 0)
    total = jnp.sum(parts, axis=0)
    return jnp.concatenate([total[:, :cols], total[:, cols:]], axis=0)


def solution(mesh):
    fine = jax.sharding.Mesh(mesh.devices.reshape(4, 2, 2, 2, 4), AXES)
    in_specs = (P(AXES, None), P(), P())
    return jax.shard_map(
        shards, mesh=fine, in_specs=in_specs, out_specs=P(AXES, None), check_vma=False
    )
```

```python
import functools
import math

import jax
import jax.numpy as jnp
import numpy as np
from jax import lax
from jax.experimental import pallas as pl
from jax.experimental.pallas import tpu as pltpu
from jax.sharding import PartitionSpec as P

NG = 96
HALF = NG // 2
SCREEN = 2.25
AXES = ("z", "x_lo", "core", "x_hi", "y")
BF = jnp.bfloat16
F32 = jnp.float32

LINES = 72
OCT = LINES // 8
MG, MI = 32, 3
CG, CI = 4, 16
ROWS = 32
CELLS = 8 * NG
WIDE = 9 * NG


def basis_table():
    index = np.arange(NG)
    phase = (index[:, None] * index[None, :]) % NG
    angle = phase.astype(np.float32) * np.float32(2.0 * math.pi / NG)
    cos_tab = np.cos(angle).astype(BF).astype(np.float32)
    sin_tab = np.sin(angle).astype(BF).astype(np.float32)
    return np.concatenate([cos_tab[:, : HALF + 1], sin_tab[:, 1:HALF]], axis=1)


def tables():
    basis = basis_table()
    ahead = np.zeros((MG, ROWS, OCT, NG), np.float32)
    for octet in range(OCT):
        for mi in range(MI):
            ahead[:, octet * MI + mi, octet, :] = basis[:, mi::MI].T
    ahead = ahead.reshape(MG * ROWS, OCT * NG)
    lane = np.arange(512).reshape(8, CG, CI)
    order = lane.transpose(1, 0, 2).reshape(-1)
    swap = np.zeros((512, 512), np.float32)
    swap[order, np.arange(512)] = 1.0
    wide = np.kron(basis, np.eye(CI, dtype=np.float32))
    x_order = (3 * np.arange(32)[None, :] + np.arange(3)[:, None]).reshape(-1)
    x_basis = basis[x_order]
    return {
        "ahead": ahead,
        "back": ahead.T,
        "swap": swap,
        "unswap": swap.T,
        "wide": wide,
        "x_ahead": x_basis.T,
        "x_back": x_basis,
    }


def const(array):
    return jnp.asarray(np.ascontiguousarray(array).astype(BF))


def mm(a, b):
    return jnp.dot(a, b, preferred_element_type=F32)


def pair_kernel(orb, rows_t, panel, ahead, swap, pair, send, fit):
    step = pl.program_id(0)
    npts = rows_t.shape[1]
    chunk, rows = 1024, 256
    totals = []
    for first in range(0, CELLS, rows):
        total = jnp.zeros((rows, 128), F32)
        for start in range(0, npts, chunk):
            corr = mm(orb[first : first + rows, :], rows_t[:, start : start + chunk])
            block = (corr * corr).astype(BF)
            pair[first : first + rows, start : start + chunk] = block
            total = total + mm(block, panel[start : start + chunk, :])
        totals.append(total)
    total = jnp.concatenate(totals, axis=0)
    low = lax.broadcasted_iota(jnp.int32, (NG, 128), 1) < 64
    for two in range(4):
        even = total[2 * two * NG : (2 * two + 1) * NG]
        odd = total[(2 * two + 1) * NG : (2 * two + 2) * NG]
        fit[pl.ds(pl.multiple_of(step * NG, NG), NG), two * 128 : (two + 1) * 128] = jnp.where(
            low, even, odd
        ).astype(BF)

    @pl.when(step == pl.num_programs(0) - 1)
    def _():
        for part in range(4):
            rows = MG * ROWS // 4
            spec = mm(ahead[part * rows : (part + 1) * rows, :], fit[...]).astype(BF)
            moved = mm(spec, swap[...]).astype(BF)
            for cg in range(CG):
                send[part * MG // 4 : (part + 1) * MG // 4, cg] = moved[
                    :, cg * 128 : (cg + 1) * 128
                ].reshape(MG // 4, ROWS, 128)


def make_pairs(orbitals, rows_t, panel2, tab):
    npts = rows_t.shape[1]
    norb = orbitals.shape[1]
    steps = orbitals.shape[0] // CELLS
    whole = lambda shape: pl.BlockSpec(shape, lambda i: (0,) * len(shape))
    return pl.pallas_call(
        pair_kernel,
        grid=(steps,),
        in_specs=[
            pl.BlockSpec((CELLS, norb), lambda i: (i, 0)),
            whole(rows_t.shape),
            whole(panel2.shape),
            whole(tab["ahead"].shape),
            whole(tab["swap"].shape),
        ],
        out_specs=[
            pl.BlockSpec((CELLS, npts), lambda i: (i, 0)),
            whole((MG, CG, ROWS, 128)),
        ],
        out_shape=[
            jax.ShapeDtypeStruct((orbitals.shape[0], npts), BF),
            jax.ShapeDtypeStruct((MG, CG, ROWS, 128), BF),
        ],
        scratch_shapes=[pltpu.VMEM((OCT * NG, 512), BF)],
        compiler_params=pltpu.CompilerParams(vmem_limit_bytes=28 * 2**20),
        name="pairs",
    )(orbitals, rows_t, panel2, const(tab["ahead"]), const(tab["swap"]))


def places():
    for part in range(4):
        for octet in range(OCT):
            for mi in range(MI):
                spot = part * OCT + octet
                yield part * ROWS + octet * MI + mi, mi, spot // 12, spot % 12


def solve_kernel(first, got, table, x_ahead, x_back, out, flat, field, wide, sem):
    fetch = pltpu.make_async_copy(table, wide, sem)
    fetch.start()
    flat[...] = got[...].astype(F32)
    for row, mi, xr, yo in places():
        field[mi, xr * 32 : (xr + 1) * 32, yo * 128 : (yo + 1) * 128] = flat[
            pl.ds(row, 32, stride=4 * ROWS), :
        ].astype(BF)
    lane = lax.broadcasted_iota(jnp.int32, (1, NG * CI), 1) // CI
    subl = lax.broadcasted_iota(jnp.int32, (NG, 1), 0)
    wave_of = lambda k: jnp.where(k <= HALF, k, k - HALF)
    weight = lambda w: jnp.where((w == 0) | (w == HALF), 1.0, 2.0).astype(F32)
    wave_y, wave_x = wave_of(lane), wave_of(subl)
    square = lambda w: w.astype(F32) * w.astype(F32)
    factor = NG / (2.0 * math.pi) * (NG / (2.0 * math.pi))
    fetch.wait()
    spec_y = mm(field[...].reshape(MI * NG, NG * CI), wide[...]).astype(BF)
    backs = []
    for mi in range(MI):
        wave_z = wave_of(first[0] + mi)
        spec = mm(x_ahead[...], spec_y[mi * NG : (mi + 1) * NG])
        total = square(wave_x) + square(wave_y) + square(wave_z)
        gain = weight(wave_x) * (weight(wave_y) * weight(wave_z))
        kernel = jnp.where(total > 0.5, factor / (total + SCREEN), 0.0) * gain
        scaled = (spec * kernel).astype(BF)
        backs.append(mm(x_back[...], scaled).astype(BF))
    plane = lax.dot_general(
        jnp.concatenate(backs, axis=0),
        wide[...],
        (((1,), (1,)), ((), ())),
        preferred_element_type=F32,
    )
    for row, mi, xr, yo in places():
        flat[pl.ds(row, 32, stride=4 * ROWS), :] = plane[
            mi * NG + xr * 32 : mi * NG + (xr + 1) * 32, yo * 128 : (yo + 1) * 128
        ]
    out[...] = flat[...].astype(BF)


def solve(first, got, tab):
    vmem = pl.BlockSpec(memory_space=pltpu.VMEM)
    return pl.pallas_call(
        solve_kernel,
        in_specs=[pl.BlockSpec(memory_space=pltpu.SMEM), vmem, pl.BlockSpec(memory_space=pl.ANY)]
        + [vmem] * 2,
        out_specs=vmem,
        out_shape=jax.ShapeDtypeStruct(got.shape, BF),
        scratch_shapes=[
            pltpu.VMEM(got.shape, F32),
            pltpu.VMEM((MI, NG, NG * CI), BF),
            pltpu.VMEM(tab["wide"].shape, BF),
            pltpu.SemaphoreType.DMA,
        ],
        compiler_params=pltpu.CompilerParams(vmem_limit_bytes=48 * 2**20),
        name="solve",
    )(
        first,
        got,
        const(tab["wide"]),
        const(tab["x_ahead"]),
        const(tab["x_back"]),
    )


def project_kernel(got, unswap, back, pair, out, spec, pot, acc, near, sems):
    steps = pair.shape[0] // WIDE
    blocks = [pl.ds(step * WIDE, WIDE) for step in range(steps)]
    copies = [
        pltpu.make_async_copy(pair.at[rows, :], near.at[rows, :], sems.at[step])
        for step, rows in enumerate(blocks)
    ]
    for copy in copies:
        copy.start()
    for part in range(4):
        rows = MG * ROWS // 4
        block = jnp.concatenate(
            [
                got[part * MG // 4 : (part + 1) * MG // 4, cg].reshape(rows, 128)
                for cg in range(CG)
            ],
            axis=1,
        )
        spec[part * rows : (part + 1) * rows, :] = mm(block, unswap[...]).astype(BF)
    for octet in range(OCT):
        final = mm(back[octet * NG : (octet + 1) * NG, :], spec[...])
        final = final / float(NG**3)
        for yi in range(8):
            start = (octet * 8 + yi) * NG
            pot[start : start + NG, :] = final[:, yi * 64 : (yi + 1) * 64].astype(BF)
    acc[...] = jnp.zeros_like(acc)
    for copy, rows in zip(copies, blocks):
        copy.wait()
        acc[...] += lax.dot_general(
            pot[rows, :], near[rows, :], (((0,), (0,)), ((), ())), preferred_element_type=F32
        )
    scale = 1.0 / math.sqrt(float(NG**3))
    turned = (acc[...] * scale).T.reshape(128, 2, 8, 64)
    out[...] = jnp.concatenate([turned[:, 0], turned[:, 1]], axis=-1)


def project(got, pair, tab):
    vmem = pl.BlockSpec(memory_space=pltpu.VMEM)
    return pl.pallas_call(
        project_kernel,
        in_specs=[vmem] * 3 + [pl.BlockSpec(memory_space=pl.ANY)],
        out_specs=vmem,
        out_shape=jax.ShapeDtypeStruct((128, 8, 128), F32),
        scratch_shapes=[
            pltpu.VMEM((MG * ROWS, 512), BF),
            pltpu.VMEM((pair.shape[0], 64), BF),
            pltpu.VMEM((64, pair.shape[1]), F32),
            pltpu.VMEM(pair.shape, BF),
            pltpu.SemaphoreType.DMA((pair.shape[0] // WIDE,)),
        ],
        compiler_params=pltpu.CompilerParams(vmem_limit_bytes=44 * 2**20),
        name="project",
    )(got, const(tab["unswap"]), const(tab["back"]), pair)


ROOM = 32
GROUP = 320


def parts_of(device):
    grid, vec = device // 8, device % 8
    return grid // 4, (vec // 4) * 2 + (grid // 2) % 2, grid % 2, vec % 4


def device_at(z, x, core, y):
    return (z * 4 + (x % 2) * 2 + core) * 8 + (x // 2) * 4 + y


def bring(data, dz=0, dx=0, dcore=0, dy=0):
    pairs = []
    for device in range(128):
        z, x, core, y = parts_of(device)
        source = device_at((z + dz) % 4, (x + dx) % 4, (core + dcore) % 2, (y + dy) % 4)
        pairs.append((source, device))
    return lax.ppermute(data, AXES, pairs)


def place_kernel(count, base, *refs):
    blocks, (slot, *more), (out, held) = refs[:count], refs[count:-2], refs[-2:]
    start = 0
    for block in blocks:
        rows = block.shape[0]
        held[start : start + rows, :] = block[...]
        start += rows
    chunk = 256
    for first in range(0, slot.shape[1], chunk):
        wanted = slot[:, first : first + chunk]
        picks = []
        for block, number in zip(blocks, base):
            index = lax.broadcasted_iota(jnp.int32, (block.shape[0], chunk), 0) + number
            picks.append(jnp.where(index == wanted, 1.0, 0.0).astype(BF))
        total = lax.dot_general(
            held[...],
            jnp.concatenate(picks, axis=0),
            (((0,), (0,)), ((), ())),
            preferred_element_type=F32,
        )
        if more:
            total = total + more[0][:, first : first + chunk].astype(F32)
        out[:, first : first + chunk] = total.astype(BF)


def place(slot, blocks, base, more=()):
    vmem = pl.BlockSpec(memory_space=pltpu.VMEM)
    norb, npts = blocks[0].shape[1], slot.shape[1]
    slots = sum(block.shape[0] for block in blocks)
    return pl.pallas_call(
        functools.partial(place_kernel, len(blocks), base),
        in_specs=[vmem] * (1 + len(blocks) + len(more)),
        out_specs=vmem,
        out_shape=jax.ShapeDtypeStruct((norb, npts), BF),
        scratch_shapes=[pltpu.VMEM((slots, norb), BF)],
        compiler_params=pltpu.CompilerParams(vmem_limit_bytes=20 * 2**20),
        cost_estimate=pl.CostEstimate(
            flops=2 * slots * norb * npts, bytes_accessed=4 * norb * npts, transcendentals=0
        ),
        name="place",
    )(*blocks, slot, *more)


def summed_rows(orbitals, points, me):
    row_count = orbitals.shape[0]
    local_pos = points - me * row_count
    inside = (local_pos >= 0) & (local_pos < row_count)
    picked = jnp.take(orbitals, jnp.clip(local_pos, 0, row_count - 1), axis=0)
    picked = jnp.where(inside[:, None], picked, jnp.zeros_like(picked)).astype(F32)
    return lax.psum(picked, AXES).astype(BF).T


def owners(points, row_count):
    return ((points.astype(F32) + 0.5) * (1.0 / row_count)).astype(jnp.int32)


def ranks(label, labels):
    size = 256
    shape = (size, size)
    early = lax.broadcasted_iota(jnp.int32, shape, 0) < lax.broadcasted_iota(jnp.int32, shape, 1)
    early = jnp.where(early, 1.0, 0.0).astype(BF)
    index = lax.broadcasted_iota(jnp.int32, (labels, size), 0)
    seen = jnp.zeros((labels, 1), F32)
    found = []
    for first in range(0, label.shape[1], size):
        match = jnp.where(index == label[:, first : first + size], 1.0, 0.0)
        before = mm(match.astype(BF), early) + seen
        found.append(jnp.sum(match * before, axis=0, keepdims=True))
        seen = seen + jnp.sum(match, axis=1, keepdims=True)
    return jnp.concatenate(found, axis=1).astype(jnp.int32), jnp.max(seen)


def lookup(key, value, first, rows):
    number = lax.broadcasted_iota(jnp.int32, (rows, 128), 0) + first
    total = jnp.zeros((rows, 128), jnp.int32)
    for start in range(0, key.shape[1], 128):
        total = total + jnp.where(
            key[:, start : start + 128] == number, value[:, start : start + 128], 0
        )
    return jnp.sum(total.astype(F32), axis=1, keepdims=True).astype(jnp.int32)


def own_kernel(me, points, orbitals, own, rank, picks, spots, near, sems, one):
    row_count = orbitals.shape[0]
    owner = owners(points[...], row_count)
    mine = owner == me[0]
    own_rank, _ = ranks(jnp.where(mine, 0, 16), 16)
    key = jnp.where(mine, own_rank, -1)
    pick = lookup(key, points[...] - me[0] * row_count, 0, ROOM)
    picks[...] = jnp.broadcast_to(pick, (ROOM, 128))
    move = pltpu.make_async_copy(picks, spots, one)
    move.start()
    move.wait()
    copies = []
    for place in range(ROOM):
        start = pl.multiple_of((spots[place, 0] >> 4) << 4, 16)
        copies.append(
            pltpu.make_async_copy(
                orbitals.at[pl.ds(start, 16), :],
                near.at[pl.ds(place * 16, 16), :],
                sems.at[place],
            )
        )
        copies[-1].start()
    rank[...] = owner
    for copy in copies:
        copy.wait()
    lane = lax.broadcasted_iota(jnp.int32, (ROOM, 16 * ROOM), 1)
    line = lax.broadcasted_iota(jnp.int32, (ROOM, 16 * ROOM), 0)
    select = jnp.where(lane == line * 16 + (pick & 15), 1.0, 0.0).astype(BF)
    own[...] = mm(select, near[...]).astype(BF)


def index_kernel(me, owner_of, fits, choose, slot):
    _, my_x, my_core, _ = parts_of(me[0])
    owner = owner_of[...]
    z, y, core = owner >> 5, owner & 3, (owner >> 3) & 1
    x = ((owner >> 2) & 1) * 2 + ((owner >> 4) & 1)
    own_rank, own_most = ranks(owner, 128)
    group_rank, group_most = ranks(x * 2 + core, 16)
    fits[0] = ((own_most <= ROOM) & (group_most <= GROUP)).astype(jnp.int32)
    spot = z * (4 * ROOM) + y * ROOM + own_rank
    key = jnp.where((x == my_x) & (core == my_core), group_rank, -1)
    for first in range(0, GROUP, 64):
        source = lookup(key, spot + 1, first, 64) - 1
        lane = lax.broadcasted_iota(jnp.int32, (64, 16 * ROOM), 1)
        choose[first : first + 64, :] = jnp.where(source == lane, 1.0, 0.0).astype(BF)
    slot[...] = (((core - my_core) & 1) * 4 + ((x - my_x) & 3)) * GROUP + group_rank


def fetch_own(me, points, orbitals):
    vmem = pl.BlockSpec(memory_space=pltpu.VMEM)
    smem = pl.BlockSpec(memory_space=pltpu.SMEM)
    npts, norb = points.shape[0], orbitals.shape[1]
    return pl.pallas_call(
        own_kernel,
        in_specs=[smem, vmem, pl.BlockSpec(memory_space=pl.ANY)],
        out_specs=[vmem, vmem],
        out_shape=[
            jax.ShapeDtypeStruct((ROOM, norb), BF),
            jax.ShapeDtypeStruct((1, npts), jnp.int32),
        ],
        scratch_shapes=[
            pltpu.VMEM((ROOM, 128), jnp.int32),
            pltpu.SMEM((ROOM, 128), jnp.int32),
            pltpu.VMEM((16 * ROOM, norb), BF),
            pltpu.SemaphoreType.DMA((ROOM,)),
            pltpu.SemaphoreType.DMA,
        ],
        compiler_params=pltpu.CompilerParams(vmem_limit_bytes=16 * 2**20),
        name="own",
    )(me.reshape(1), points[None], orbitals)


def index(me, owner):
    vmem = pl.BlockSpec(memory_space=pltpu.VMEM)
    smem = pl.BlockSpec(memory_space=pltpu.SMEM)
    return pl.pallas_call(
        index_kernel,
        in_specs=[smem, vmem],
        out_specs=[smem, vmem, vmem],
        out_shape=[
            jax.ShapeDtypeStruct((1,), jnp.int32),
            jax.ShapeDtypeStruct((GROUP, 16 * ROOM), BF),
            jax.ShapeDtypeStruct(owner.shape, jnp.int32),
        ],
        compiler_params=pltpu.CompilerParams(vmem_limit_bytes=16 * 2**20),
        cost_estimate=pl.CostEstimate(
            flops=3 * 10**9, bytes_accessed=10**7, transcendentals=0
        ),
        name="index",
    )(me.reshape(1), owner)


def spread_rows(held, slot):
    mate = lambda block: bring(block, dcore=1)
    half, ring = GROUP // 2, 4 * GROUP
    right, left = bring(held, dx=1), bring(held, dx=3)
    rows = place(slot, [held, mate(held)], (0, ring))
    far_a, far_b = bring(right[:half], dx=1), bring(left[half:], dx=3)
    near = [right, left, mate(right), mate(left)]
    rows = place(slot, near, (GROUP, 3 * GROUP, ring + GROUP, ring + 3 * GROUP), (rows,))
    far_a, far_b, rows = lax.optimization_barrier((far_a, far_b, rows))
    far = [far_a, far_b, mate(far_a), mate(far_b)]
    start = 2 * GROUP
    return place(slot, far, (start, start + half, ring + start, ring + start + half), (rows,))


def gather_rows(orbitals, points, me):
    own, owner = fetch_own(me, points, orbitals)
    copies = jnp.broadcast_to(own[None], (16,) + own.shape)
    square = lax.all_to_all(copies, ("z", "y"), 0, 0).reshape(16 * ROOM, own.shape[1])
    fits, choose, slot = index(me, owner)
    held = mm(choose, square).astype(BF)
    return lax.cond(
        fits[0] > 0,
        lambda: spread_rows(held, slot),
        lambda: summed_rows(orbitals, points, me),
    )


def shards(orbitals, inverse_panel, points):
    tab = tables()
    devices = lax.axis_size(AXES)
    me = lax.axis_index(AXES)
    npoints, cols = inverse_panel.shape
    rows_t = gather_rows(orbitals, points, me)
    panel2 = jnp.concatenate([inverse_panel, inverse_panel], axis=1)
    pair, send = make_pairs(orbitals, rows_t, panel2, tab)
    planes = lax.all_to_all(send.reshape(devices, ROWS, 128), AXES, 0, 0)
    first = (me // CG * MI).astype(jnp.int32).reshape(1)
    ret = solve(first, planes.reshape(devices * ROWS, 128), tab)
    got = lax.all_to_all(ret.reshape(devices, ROWS, 128), AXES, 0, 0)
    parts = project(got.reshape(MG, CG, ROWS, 128), pair, tab)
    parts = lax.all_to_all(parts, AXES, 0, 0)
    total = jnp.sum(parts, axis=0)
    return jnp.concatenate([total[:, :cols], total[:, cols:]], axis=0)


def solution(mesh):
    fine = jax.sharding.Mesh(mesh.devices.reshape(4, 2, 2, 2, 4), AXES)
    in_specs = (P(AXES, None), P(), P())
    return jax.shard_map(
        shards, mesh=fine, in_specs=in_specs, out_specs=P(AXES, None), check_vma=False
    )
```

```python
import functools
import math

import jax
import jax.numpy as jnp
import numpy as np
from jax import lax
from jax.experimental import pallas as pl
from jax.experimental.pallas import tpu as pltpu
from jax.sharding import PartitionSpec as P

NG = 96
HALF = NG // 2
SCREEN = 2.25
AXES = ("z", "x_lo", "core", "x_hi", "y")
BF = jnp.bfloat16
F32 = jnp.float32

LINES = 72
OCT = LINES // 8
MG, MI = 32, 3
CG, CI = 4, 16
ROWS = 32
ROOM = 32
GROUP = 320
HALF_GROUP = GROUP // 2
FAR = (2 * GROUP, 2 * GROUP + HALF_GROUP, 6 * GROUP, 6 * GROUP + HALF_GROUP)
CELLS = 8 * NG
WIDE = 9 * NG


def basis_table():
    index = np.arange(NG)
    phase = (index[:, None] * index[None, :]) % NG
    angle = phase.astype(np.float32) * np.float32(2.0 * math.pi / NG)
    cos_tab = np.cos(angle).astype(BF).astype(np.float32)
    sin_tab = np.sin(angle).astype(BF).astype(np.float32)
    return np.concatenate([cos_tab[:, : HALF + 1], sin_tab[:, 1:HALF]], axis=1)


def tables():
    basis = basis_table()
    ahead = np.zeros((MG, ROWS, OCT, NG), np.float32)
    for octet in range(OCT):
        for mi in range(MI):
            ahead[:, octet * MI + mi, octet, :] = basis[:, mi::MI].T
    ahead = ahead.reshape(MG * ROWS, OCT * NG)
    lane = np.arange(512).reshape(8, CG, CI)
    order = lane.transpose(1, 0, 2).reshape(-1)
    swap = np.zeros((512, 512), np.float32)
    swap[order, np.arange(512)] = 1.0
    wide = np.kron(basis, np.eye(CI, dtype=np.float32))
    x_order = (3 * np.arange(32)[None, :] + np.arange(3)[:, None]).reshape(-1)
    x_basis = basis[x_order]
    return {
        "ahead": ahead,
        "back": ahead.T,
        "swap": swap,
        "unswap": swap.T,
        "wide": wide,
        "x_ahead": x_basis.T,
        "x_back": x_basis,
    }


def const(array):
    return jnp.asarray(np.ascontiguousarray(array).astype(BF))


def mm(a, b):
    return jnp.dot(a, b, preferred_element_type=F32)


def pair_kernel(
    orb, part_t, slot, far0, far1, far2, far3, panel, ahead, swap, pair, send, fit, rows_t, held
):
    step = pl.program_id(0)

    @pl.when(step == 0)
    def _():
        fill(FAR, (far0, far1, far2, far3), slot, (part_t,), held, rows_t)

    npts = rows_t.shape[1]
    chunk, rows = 1024, 256
    totals = []
    for first in range(0, CELLS, rows):
        total = jnp.zeros((rows, 128), F32)
        for start in range(0, npts, chunk):
            corr = mm(orb[first : first + rows, :], rows_t[:, start : start + chunk])
            block = (corr * corr).astype(BF)
            pair[first : first + rows, start : start + chunk] = block
            total = total + mm(block, panel[start : start + chunk, :])
        totals.append(total)
    total = jnp.concatenate(totals, axis=0)
    low = lax.broadcasted_iota(jnp.int32, (NG, 128), 1) < 64
    for two in range(4):
        even = total[2 * two * NG : (2 * two + 1) * NG]
        odd = total[(2 * two + 1) * NG : (2 * two + 2) * NG]
        fit[pl.ds(pl.multiple_of(step * NG, NG), NG), two * 128 : (two + 1) * 128] = jnp.where(
            low, even, odd
        ).astype(BF)

    @pl.when(step == pl.num_programs(0) - 1)
    def _():
        for part in range(4):
            rows = MG * ROWS // 4
            spec = mm(ahead[part * rows : (part + 1) * rows, :], fit[...]).astype(BF)
            moved = mm(spec, swap[...]).astype(BF)
            for cg in range(CG):
                send[part * MG // 4 : (part + 1) * MG // 4, cg] = moved[
                    :, cg * 128 : (cg + 1) * 128
                ].reshape(MG // 4, ROWS, 128)


def make_pairs(orbitals, part_t, slot, far, panel2, tab):
    npts = part_t.shape[1]
    norb = orbitals.shape[1]
    steps = orbitals.shape[0] // CELLS
    whole = lambda shape: pl.BlockSpec(shape, lambda i: (0,) * len(shape))
    return pl.pallas_call(
        pair_kernel,
        grid=(steps,),
        in_specs=[
            pl.BlockSpec((CELLS, norb), lambda i: (i, 0)),
            whole(part_t.shape),
            whole(slot.shape),
            *[whole(block.shape) for block in far],
            whole(panel2.shape),
            whole(tab["ahead"].shape),
            whole(tab["swap"].shape),
        ],
        out_specs=[
            pl.BlockSpec((CELLS, npts), lambda i: (i, 0)),
            whole((MG, CG, ROWS, 128)),
        ],
        out_shape=[
            jax.ShapeDtypeStruct((orbitals.shape[0], npts), BF),
            jax.ShapeDtypeStruct((MG, CG, ROWS, 128), BF),
        ],
        scratch_shapes=[
            pltpu.VMEM((OCT * NG, 512), BF),
            pltpu.VMEM(part_t.shape, BF),
            pltpu.VMEM((4 * HALF_GROUP, norb), BF),
        ],
        compiler_params=pltpu.CompilerParams(vmem_limit_bytes=36 * 2**20),
        name="pairs",
    )(orbitals, part_t, slot, *far, panel2, const(tab["ahead"]), const(tab["swap"]))


def places():
    for part in range(4):
        for octet in range(OCT):
            for mi in range(MI):
                spot = part * OCT + octet
                yield part * ROWS + octet * MI + mi, mi, spot // 12, spot % 12


def solve_kernel(me, got, table, x_ahead, x_back, out, flat, field, wide, sem):
    fetch = pltpu.make_async_copy(table, wide, sem)
    fetch.start()
    flat[...] = got[...].astype(F32)
    for row, mi, xr, yo in places():
        field[mi, xr * 32 : (xr + 1) * 32, yo * 128 : (yo + 1) * 128] = flat[
            pl.ds(row, 32, stride=4 * ROWS), :
        ].astype(BF)
    lane = lax.broadcasted_iota(jnp.int32, (1, NG * CI), 1) // CI
    subl = lax.broadcasted_iota(jnp.int32, (NG, 1), 0)
    wave_of = lambda k: jnp.where(k <= HALF, k, k - HALF)
    weight = lambda w: jnp.where((w == 0) | (w == HALF), 1.0, 2.0).astype(F32)
    wave_y, wave_x = wave_of(lane), wave_of(subl)
    square = lambda w: w.astype(F32) * w.astype(F32)
    factor = NG / (2.0 * math.pi) * (NG / (2.0 * math.pi))
    fetch.wait()
    spec_y = mm(field[...].reshape(MI * NG, NG * CI), wide[...]).astype(BF)
    backs = []
    for mi in range(MI):
        wave_z = wave_of((me[0] >> 2) * MI + mi)
        spec = mm(x_ahead[...], spec_y[mi * NG : (mi + 1) * NG])
        total = square(wave_x) + square(wave_y) + square(wave_z)
        gain = weight(wave_x) * (weight(wave_y) * weight(wave_z))
        kernel = jnp.where(total > 0.5, factor / (total + SCREEN), 0.0) * gain
        scaled = (spec * kernel).astype(BF)
        backs.append(mm(x_back[...], scaled).astype(BF))
    plane = lax.dot_general(
        jnp.concatenate(backs, axis=0),
        wide[...],
        (((1,), (1,)), ((), ())),
        preferred_element_type=F32,
    )
    for row, mi, xr, yo in places():
        flat[pl.ds(row, 32, stride=4 * ROWS), :] = plane[
            mi * NG + xr * 32 : mi * NG + (xr + 1) * 32, yo * 128 : (yo + 1) * 128
        ]
    out[...] = flat[...].astype(BF)


def solve(me, got, tab):
    vmem = pl.BlockSpec(memory_space=pltpu.VMEM)
    return pl.pallas_call(
        solve_kernel,
        in_specs=[pl.BlockSpec(memory_space=pltpu.SMEM), vmem, pl.BlockSpec(memory_space=pl.ANY)]
        + [vmem] * 2,
        out_specs=vmem,
        out_shape=jax.ShapeDtypeStruct(got.shape, BF),
        scratch_shapes=[
            pltpu.VMEM(got.shape, F32),
            pltpu.VMEM((MI, NG, NG * CI), BF),
            pltpu.VMEM(tab["wide"].shape, BF),
            pltpu.SemaphoreType.DMA,
        ],
        compiler_params=pltpu.CompilerParams(vmem_limit_bytes=48 * 2**20),
        name="solve",
    )(
        me,
        got,
        const(tab["wide"]),
        const(tab["x_ahead"]),
        const(tab["x_back"]),
    )


def project_kernel(got, unswap, back, pair, out, spec, pot, acc, near, sems):
    steps = pair.shape[0] // WIDE
    blocks = [pl.ds(step * WIDE, WIDE) for step in range(steps)]
    copies = [
        pltpu.make_async_copy(pair.at[rows, :], near.at[rows, :], sems.at[step])
        for step, rows in enumerate(blocks)
    ]
    for copy in copies:
        copy.start()
    for part in range(4):
        rows = MG * ROWS // 4
        block = jnp.concatenate(
            [
                got[part * MG // 4 : (part + 1) * MG // 4, cg].reshape(rows, 128)
                for cg in range(CG)
            ],
            axis=1,
        )
        spec[part * rows : (part + 1) * rows, :] = mm(block, unswap[...]).astype(BF)
    for octet in range(OCT):
        final = mm(back[octet * NG : (octet + 1) * NG, :], spec[...])
        final = final / float(NG**3)
        for yi in range(8):
            start = (octet * 8 + yi) * NG
            pot[start : start + NG, :] = final[:, yi * 64 : (yi + 1) * 64].astype(BF)
    acc[...] = jnp.zeros_like(acc)
    for copy, rows in zip(copies, blocks):
        copy.wait()
        acc[...] += lax.dot_general(
            pot[rows, :], near[rows, :], (((0,), (0,)), ((), ())), preferred_element_type=F32
        )
    scale = 1.0 / math.sqrt(float(NG**3))
    turned = (acc[...] * scale).T.reshape(128, 2, 8, 64)
    out[...] = jnp.concatenate([turned[:, 0], turned[:, 1]], axis=-1)


def project(got, pair, tab):
    vmem = pl.BlockSpec(memory_space=pltpu.VMEM)
    return pl.pallas_call(
        project_kernel,
        in_specs=[vmem] * 3 + [pl.BlockSpec(memory_space=pl.ANY)],
        out_specs=vmem,
        out_shape=jax.ShapeDtypeStruct((128, 8, 128), F32),
        scratch_shapes=[
            pltpu.VMEM((MG * ROWS, 512), BF),
            pltpu.VMEM((pair.shape[0], 64), BF),
            pltpu.VMEM((64, pair.shape[1]), F32),
            pltpu.VMEM(pair.shape, BF),
            pltpu.SemaphoreType.DMA((pair.shape[0] // WIDE,)),
        ],
        compiler_params=pltpu.CompilerParams(vmem_limit_bytes=44 * 2**20),
        name="project",
    )(got, const(tab["unswap"]), const(tab["back"]), pair)


def parts_of(device):
    grid, vec = device // 8, device % 8
    return grid // 4, (vec // 4) * 2 + (grid // 2) % 2, grid % 2, vec % 4


def device_at(z, x, core, y):
    return (z * 4 + (x % 2) * 2 + core) * 8 + (x // 2) * 4 + y


def bring(data, dz=0, dx=0, dcore=0, dy=0):
    pairs = []
    for device in range(128):
        z, x, core, y = parts_of(device)
        source = device_at((z + dz) % 4, (x + dx) % 4, (core + dcore) % 2, (y + dy) % 4)
        pairs.append((source, device))
    return lax.ppermute(data, AXES, pairs)


def fill(base, blocks, slot, more, held, out):
    start = 0
    for block in blocks:
        rows = block.shape[0]
        held[start : start + rows, :] = block[...]
        start += rows
    chunk = 256
    for first in range(0, slot.shape[1], chunk):
        wanted = slot[:, first : first + chunk]
        picks = []
        for block, number in zip(blocks, base):
            index = lax.broadcasted_iota(jnp.int32, (block.shape[0], chunk), 0) + number
            picks.append(jnp.where(index == wanted, 1.0, 0.0).astype(BF))
        total = lax.dot_general(
            held[...],
            jnp.concatenate(picks, axis=0),
            (((0,), (0,)), ((), ())),
            preferred_element_type=F32,
        )
        if more:
            total = total + more[0][:, first : first + chunk].astype(F32)
        out[:, first : first + chunk] = total.astype(BF)


def place_kernel(count, base, *refs):
    blocks, (slot, *more), (out, held) = refs[:count], refs[count:-2], refs[-2:]
    fill(base, blocks, slot, more, held, out)


def place(slot, blocks, base, more=()):
    vmem = pl.BlockSpec(memory_space=pltpu.VMEM)
    norb, npts = blocks[0].shape[1], slot.shape[1]
    slots = sum(block.shape[0] for block in blocks)
    return pl.pallas_call(
        functools.partial(place_kernel, len(blocks), base),
        in_specs=[vmem] * (1 + len(blocks) + len(more)),
        out_specs=vmem,
        out_shape=jax.ShapeDtypeStruct((norb, npts), BF),
        scratch_shapes=[pltpu.VMEM((slots, norb), BF)],
        compiler_params=pltpu.CompilerParams(vmem_limit_bytes=20 * 2**20),
        cost_estimate=pl.CostEstimate(
            flops=2 * slots * norb * npts, bytes_accessed=4 * norb * npts, transcendentals=0
        ),
        name="place",
    )(*blocks, slot, *more)


def summed_rows(orbitals, points, me):
    row_count = orbitals.shape[0]
    local_pos = points - me * row_count
    inside = (local_pos >= 0) & (local_pos < row_count)
    picked = jnp.take(orbitals, jnp.clip(local_pos, 0, row_count - 1), axis=0)
    picked = jnp.where(inside[:, None], picked, jnp.zeros_like(picked)).astype(F32)
    return lax.psum(picked, AXES).astype(BF).T


def owners(points, row_count):
    return ((points.astype(F32) + 0.5) * (1.0 / row_count)).astype(jnp.int32)


def ranks(label, labels):
    size = 256
    shape = (size, size)
    early = lax.broadcasted_iota(jnp.int32, shape, 0) < lax.broadcasted_iota(jnp.int32, shape, 1)
    early = jnp.where(early, 1.0, 0.0).astype(BF)
    index = lax.broadcasted_iota(jnp.int32, (labels, size), 0)
    seen = jnp.zeros((labels, 1), F32)
    found = []
    for first in range(0, label.shape[1], size):
        match = jnp.where(index == label[:, first : first + size], 1.0, 0.0)
        before = mm(match.astype(BF), early) + seen
        found.append(jnp.sum(match * before, axis=0, keepdims=True))
        seen = seen + jnp.sum(match, axis=1, keepdims=True)
    return jnp.concatenate(found, axis=1).astype(jnp.int32), jnp.max(seen)


def lookup(key, value, first, rows):
    number = lax.broadcasted_iota(jnp.int32, (rows, 128), 0) + first
    total = jnp.zeros((rows, 128), jnp.int32)
    for start in range(0, key.shape[1], 128):
        total = total + jnp.where(
            key[:, start : start + 128] == number, value[:, start : start + 128], 0
        )
    return jnp.sum(total.astype(F32), axis=1, keepdims=True).astype(jnp.int32)


def own_kernel(me, points, orbitals, own, rank, picks, spots, near, sems, one):
    row_count = orbitals.shape[0]
    owner = owners(points[...], row_count)
    mine = owner == me[0]
    own_rank, _ = ranks(jnp.where(mine, 0, 16), 16)
    key = jnp.where(mine, own_rank, -1)
    pick = lookup(key, points[...] - me[0] * row_count, 0, ROOM)
    picks[...] = jnp.broadcast_to(pick, (ROOM, 128))
    move = pltpu.make_async_copy(picks, spots, one)
    move.start()
    move.wait()
    copies = []
    for place in range(ROOM):
        start = pl.multiple_of((spots[place, 0] >> 4) << 4, 16)
        copies.append(
            pltpu.make_async_copy(
                orbitals.at[pl.ds(start, 16), :],
                near.at[pl.ds(place * 16, 16), :],
                sems.at[place],
            )
        )
        copies[-1].start()
    rank[...] = owner
    for copy in copies:
        copy.wait()
    lane = lax.broadcasted_iota(jnp.int32, (ROOM, 16 * ROOM), 1)
    line = lax.broadcasted_iota(jnp.int32, (ROOM, 16 * ROOM), 0)
    select = jnp.where(lane == line * 16 + (pick & 15), 1.0, 0.0).astype(BF)
    own[...] = mm(select, near[...]).astype(BF)


def index_kernel(me, owner_of, fits, choose, slot):
    _, my_x, my_core, _ = parts_of(me[0])
    owner = owner_of[...]
    z, y, core = owner >> 5, owner & 3, (owner >> 3) & 1
    x = ((owner >> 2) & 1) * 2 + ((owner >> 4) & 1)
    own_rank, own_most = ranks(owner, 128)
    group_rank, group_most = ranks(x * 2 + core, 16)
    fit = (own_most <= ROOM) & (group_most <= GROUP)
    fits[0] = fit.astype(jnp.int32)
    spot = z * (4 * ROOM) + y * ROOM + own_rank
    key = jnp.where((x == my_x) & (core == my_core), group_rank, -1)
    for first in range(0, GROUP, 64):
        source = lookup(key, spot + 1, first, 64) - 1
        lane = lax.broadcasted_iota(jnp.int32, (64, 16 * ROOM), 1)
        choose[first : first + 64, :] = jnp.where(source == lane, 1.0, 0.0).astype(BF)
    number = (((core - my_core) & 1) * 4 + ((x - my_x) & 3)) * GROUP + group_rank
    slot[...] = jnp.where(fit, number, -1)


def fetch_own(me, points, orbitals):
    vmem = pl.BlockSpec(memory_space=pltpu.VMEM)
    smem = pl.BlockSpec(memory_space=pltpu.SMEM)
    npts, norb = points.shape[0], orbitals.shape[1]
    return pl.pallas_call(
        own_kernel,
        in_specs=[smem, vmem, pl.BlockSpec(memory_space=pl.ANY)],
        out_specs=[vmem, vmem],
        out_shape=[
            jax.ShapeDtypeStruct((ROOM, norb), BF),
            jax.ShapeDtypeStruct((1, npts), jnp.int32),
        ],
        scratch_shapes=[
            pltpu.VMEM((ROOM, 128), jnp.int32),
            pltpu.SMEM((ROOM, 128), jnp.int32),
            pltpu.VMEM((16 * ROOM, norb), BF),
            pltpu.SemaphoreType.DMA((ROOM,)),
            pltpu.SemaphoreType.DMA,
        ],
        compiler_params=pltpu.CompilerParams(vmem_limit_bytes=16 * 2**20),
        name="own",
    )(me.reshape(1), points[None], orbitals)


def index(me, owner):
    vmem = pl.BlockSpec(memory_space=pltpu.VMEM)
    smem = pl.BlockSpec(memory_space=pltpu.SMEM)
    return pl.pallas_call(
        index_kernel,
        in_specs=[smem, vmem],
        out_specs=[smem, vmem, vmem],
        out_shape=[
            jax.ShapeDtypeStruct((1,), jnp.int32),
            jax.ShapeDtypeStruct((GROUP, 16 * ROOM), BF),
            jax.ShapeDtypeStruct(owner.shape, jnp.int32),
        ],
        compiler_params=pltpu.CompilerParams(vmem_limit_bytes=16 * 2**20),
        cost_estimate=pl.CostEstimate(
            flops=3 * 10**9, bytes_accessed=10**7, transcendentals=0
        ),
        name="index",
    )(me.reshape(1), owner)


def spread_rows(held, slot):
    mate = lambda block: bring(block, dcore=1)
    half, ring = GROUP // 2, 4 * GROUP
    right, left = bring(held, dx=1), bring(held, dx=3)
    rows = place(slot, [held, mate(held)], (0, ring))
    far_a, far_b = bring(right[:half], dx=1), bring(left[half:], dx=3)
    near = [right, left, mate(right), mate(left)]
    rows = place(slot, near, (GROUP, 3 * GROUP, ring + GROUP, ring + 3 * GROUP), (rows,))
    far_a, far_b, rows = lax.optimization_barrier((far_a, far_b, rows))
    return rows, far_a, far_b, mate(far_a), mate(far_b)


def gather_rows(orbitals, points, me):
    own, owner = fetch_own(me, points, orbitals)
    copies = jnp.broadcast_to(own[None], (16,) + own.shape)
    square = lax.all_to_all(copies, ("z", "y"), 0, 0).reshape(16 * ROOM, own.shape[1])
    fits, choose, slot = index(me, owner)
    held = mm(choose, square).astype(BF)
    none = jnp.zeros((HALF_GROUP, orbitals.shape[1]), BF)
    rows, *far = lax.cond(
        fits[0] > 0,
        lambda: spread_rows(held, slot),
        lambda: (summed_rows(orbitals, points, me), none, none, none, none),
    )
    return rows, slot, far


def shards(orbitals, inverse_panel, points):
    tab = tables()
    devices = lax.axis_size(AXES)
    me = lax.axis_index(AXES)
    npoints, cols = inverse_panel.shape
    part_t, slot, far = gather_rows(orbitals, points, me)
    panel2 = jnp.concatenate([inverse_panel, inverse_panel], axis=1)
    pair, send = make_pairs(orbitals, part_t, slot, far, panel2, tab)
    planes = lax.all_to_all(send.reshape(devices, ROWS, 128), AXES, 0, 0)
    ret = solve(me.reshape(1), planes.reshape(devices * ROWS, 128), tab)
    got = lax.all_to_all(ret.reshape(devices, ROWS, 128), AXES, 0, 0)
    parts = project(got.reshape(MG, CG, ROWS, 128), pair, tab)
    parts = lax.all_to_all(parts, AXES, 0, 0)
    total = jnp.sum(parts, axis=0)
    return jnp.concatenate([total[:, :cols], total[:, cols:]], axis=0)


def solution(mesh):
    fine = jax.sharding.Mesh(mesh.devices.reshape(4, 2, 2, 2, 4), AXES)
    in_specs = (P(AXES, None), P(), P())
    return jax.shard_map(
        shards, mesh=fine, in_specs=in_specs, out_specs=P(AXES, None), check_vma=False
    )
```

```python
import functools
import math

import jax
import jax.numpy as jnp
import numpy as np
from jax import lax
from jax.experimental import pallas as pl
from jax.experimental.pallas import tpu as pltpu
from jax.sharding import PartitionSpec as P

NG = 96
HALF = NG // 2
SCREEN = 2.25
AXES = ("z", "x_lo", "core", "x_hi", "y")
BF = jnp.bfloat16
F32 = jnp.float32

LINES = 72
OCT = LINES // 8
MG, MI = 32, 3
CG, CI = 4, 16
ROWS = 32
ROOM = 32
GROUP = 320
HALF_GROUP = GROUP // 2
FAR = (2 * GROUP, 2 * GROUP + HALF_GROUP, 6 * GROUP, 6 * GROUP + HALF_GROUP)
CELLS = 8 * NG
WIDE = 9 * NG


def basis_table():
    index = np.arange(NG)
    phase = (index[:, None] * index[None, :]) % NG
    angle = phase.astype(np.float32) * np.float32(2.0 * math.pi / NG)
    cos_tab = np.cos(angle).astype(BF).astype(np.float32)
    sin_tab = np.sin(angle).astype(BF).astype(np.float32)
    return np.concatenate([cos_tab[:, : HALF + 1], sin_tab[:, 1:HALF]], axis=1)


def tables():
    basis = basis_table()
    ahead = np.zeros((MG, ROWS, OCT, NG), np.float32)
    for octet in range(OCT):
        for mi in range(MI):
            ahead[:, octet * MI + mi, octet, :] = basis[:, mi::MI].T
    ahead = ahead.reshape(MG * ROWS, OCT * NG)
    lane = np.arange(512).reshape(8, CG, CI)
    order = lane.transpose(1, 0, 2).reshape(-1)
    swap = np.zeros((512, 512), np.float32)
    swap[order, np.arange(512)] = 1.0
    wide = np.kron(basis, np.eye(CI, dtype=np.float32))
    x_order = (3 * np.arange(32)[None, :] + np.arange(3)[:, None]).reshape(-1)
    x_basis = basis[x_order]
    return {
        "ahead": ahead,
        "back": ahead.T,
        "swap": swap,
        "unswap": swap.T,
        "wide": wide,
        "x_ahead": x_basis.T,
        "x_back": x_basis,
    }


def const(array):
    return jnp.asarray(np.ascontiguousarray(array).astype(BF))


def mm(a, b):
    return jnp.dot(a, b, preferred_element_type=F32)


def pair_kernel(fits, spare, orb, part_t, slot, far0, far1, far2, far3, *refs):
    panel, ahead, swap, pair, send, fit, rows_t, held, sem = refs
    step = pl.program_id(0)

    @pl.when((step == 0) & (fits[0] > 0))
    def _():
        fill(FAR, (far0, far1, far2, far3), slot, (part_t,), held, rows_t)

    @pl.when((step == 0) & (fits[0] <= 0))
    def _():
        copy = pltpu.make_async_copy(spare, rows_t, sem)
        copy.start()
        copy.wait()

    npts = rows_t.shape[1]
    chunk, rows = 1024, 256
    totals = []
    for first in range(0, CELLS, rows):
        total = jnp.zeros((rows, 128), F32)
        for start in range(0, npts, chunk):
            corr = mm(orb[first : first + rows, :], rows_t[:, start : start + chunk])
            block = (corr * corr).astype(BF)
            pair[first : first + rows, start : start + chunk] = block
            total = total + mm(block, panel[start : start + chunk, :])
        totals.append(total)
    total = jnp.concatenate(totals, axis=0)
    low = lax.broadcasted_iota(jnp.int32, (NG, 128), 1) < 64
    for two in range(4):
        even = total[2 * two * NG : (2 * two + 1) * NG]
        odd = total[(2 * two + 1) * NG : (2 * two + 2) * NG]
        fit[pl.ds(pl.multiple_of(step * NG, NG), NG), two * 128 : (two + 1) * 128] = jnp.where(
            low, even, odd
        ).astype(BF)

    @pl.when(step == pl.num_programs(0) - 1)
    def _():
        for part in range(4):
            rows = MG * ROWS // 4
            spec = mm(ahead[part * rows : (part + 1) * rows, :], fit[...]).astype(BF)
            moved = mm(spec, swap[...]).astype(BF)
            for cg in range(CG):
                send[part * MG // 4 : (part + 1) * MG // 4, cg] = moved[
                    :, cg * 128 : (cg + 1) * 128
                ].reshape(MG // 4, ROWS, 128)


def make_pairs(fits, spare, orbitals, part_t, slot, far, panel2, tab):
    npts = part_t.shape[1]
    norb = orbitals.shape[1]
    steps = orbitals.shape[0] // CELLS
    whole = lambda shape: pl.BlockSpec(shape, lambda i: (0,) * len(shape))
    return pl.pallas_call(
        pair_kernel,
        grid=(steps,),
        in_specs=[
            pl.BlockSpec(memory_space=pltpu.SMEM),
            pl.BlockSpec(memory_space=pl.ANY),
            pl.BlockSpec((CELLS, norb), lambda i: (i, 0)),
            whole(part_t.shape),
            whole(slot.shape),
            *[whole(block.shape) for block in far],
            whole(panel2.shape),
            whole(tab["ahead"].shape),
            whole(tab["swap"].shape),
        ],
        out_specs=[
            pl.BlockSpec((CELLS, npts), lambda i: (i, 0)),
            whole((MG, CG, ROWS, 128)),
        ],
        out_shape=[
            jax.ShapeDtypeStruct((orbitals.shape[0], npts), BF),
            jax.ShapeDtypeStruct((MG, CG, ROWS, 128), BF),
        ],
        scratch_shapes=[
            pltpu.VMEM((OCT * NG, 512), BF),
            pltpu.VMEM(part_t.shape, BF),
            pltpu.VMEM((4 * HALF_GROUP, norb), BF),
            pltpu.SemaphoreType.DMA,
        ],
        compiler_params=pltpu.CompilerParams(vmem_limit_bytes=54 * 2**20),
        name="pairs",
    )(fits, spare, orbitals, part_t, slot, *far, panel2, const(tab["ahead"]), const(tab["swap"]))


def places():
    for part in range(4):
        for octet in range(OCT):
            for mi in range(MI):
                spot = part * OCT + octet
                yield part * ROWS + octet * MI + mi, mi, spot // 12, spot % 12


def solve_kernel(me, got, table, x_ahead, x_back, out, flat, field, wide, sem):
    fetch = pltpu.make_async_copy(table, wide, sem)
    fetch.start()
    flat[...] = got[...].astype(F32)
    for row, mi, xr, yo in places():
        field[mi, xr * 32 : (xr + 1) * 32, yo * 128 : (yo + 1) * 128] = flat[
            pl.ds(row, 32, stride=4 * ROWS), :
        ].astype(BF)
    lane = lax.broadcasted_iota(jnp.int32, (1, NG * CI), 1) // CI
    subl = lax.broadcasted_iota(jnp.int32, (NG, 1), 0)
    wave_of = lambda k: jnp.where(k <= HALF, k, k - HALF)
    weight = lambda w: jnp.where((w == 0) | (w == HALF), 1.0, 2.0).astype(F32)
    wave_y, wave_x = wave_of(lane), wave_of(subl)
    square = lambda w: w.astype(F32) * w.astype(F32)
    factor = NG / (2.0 * math.pi) * (NG / (2.0 * math.pi))
    fetch.wait()
    spec_y = mm(field[...].reshape(MI * NG, NG * CI), wide[...]).astype(BF)
    backs = []
    for mi in range(MI):
        wave_z = wave_of((me[0] >> 2) * MI + mi)
        spec = mm(x_ahead[...], spec_y[mi * NG : (mi + 1) * NG])
        total = square(wave_x) + square(wave_y) + square(wave_z)
        gain = weight(wave_x) * (weight(wave_y) * weight(wave_z))
        kernel = jnp.where(total > 0.5, factor / (total + SCREEN), 0.0) * gain
        scaled = (spec * kernel).astype(BF)
        backs.append(mm(x_back[...], scaled).astype(BF))
    plane = lax.dot_general(
        jnp.concatenate(backs, axis=0),
        wide[...],
        (((1,), (1,)), ((), ())),
        preferred_element_type=F32,
    )
    for row, mi, xr, yo in places():
        flat[pl.ds(row, 32, stride=4 * ROWS), :] = plane[
            mi * NG + xr * 32 : mi * NG + (xr + 1) * 32, yo * 128 : (yo + 1) * 128
        ]
    out[...] = flat[...].astype(BF)


def solve(me, got, tab):
    vmem = pl.BlockSpec(memory_space=pltpu.VMEM)
    return pl.pallas_call(
        solve_kernel,
        in_specs=[pl.BlockSpec(memory_space=pltpu.SMEM), vmem, pl.BlockSpec(memory_space=pl.ANY)]
        + [vmem] * 2,
        out_specs=vmem,
        out_shape=jax.ShapeDtypeStruct(got.shape, BF),
        scratch_shapes=[
            pltpu.VMEM(got.shape, F32),
            pltpu.VMEM((MI, NG, NG * CI), BF),
            pltpu.VMEM(tab["wide"].shape, BF),
            pltpu.SemaphoreType.DMA,
        ],
        compiler_params=pltpu.CompilerParams(vmem_limit_bytes=48 * 2**20),
        name="solve",
    )(
        me,
        got,
        const(tab["wide"]),
        const(tab["x_ahead"]),
        const(tab["x_back"]),
    )


def project_kernel(got, unswap, back, pair, out, spec, pot, acc, near, sems):
    steps = pair.shape[0] // WIDE
    blocks = [pl.ds(step * WIDE, WIDE) for step in range(steps)]
    copies = [
        pltpu.make_async_copy(pair.at[rows, :], near.at[rows, :], sems.at[step])
        for step, rows in enumerate(blocks)
    ]
    for copy in copies:
        copy.start()
    for part in range(4):
        rows = MG * ROWS // 4
        block = jnp.concatenate(
            [
                got[part * MG // 4 : (part + 1) * MG // 4, cg].reshape(rows, 128)
                for cg in range(CG)
            ],
            axis=1,
        )
        spec[part * rows : (part + 1) * rows, :] = mm(block, unswap[...]).astype(BF)
    for octet in range(OCT):
        final = mm(back[octet * NG : (octet + 1) * NG, :], spec[...])
        final = final / float(NG**3)
        for yi in range(8):
            start = (octet * 8 + yi) * NG
            pot[start : start + NG, :] = final[:, yi * 64 : (yi + 1) * 64].astype(BF)
    acc[...] = jnp.zeros_like(acc)
    for copy, rows in zip(copies, blocks):
        copy.wait()
        acc[...] += lax.dot_general(
            pot[rows, :], near[rows, :], (((0,), (0,)), ((), ())), preferred_element_type=F32
        )
    scale = 1.0 / math.sqrt(float(NG**3))
    turned = (acc[...] * scale).T.reshape(128, 2, 8, 64)
    out[...] = jnp.concatenate([turned[:, 0], turned[:, 1]], axis=-1)


def project(got, pair, tab):
    vmem = pl.BlockSpec(memory_space=pltpu.VMEM)
    return pl.pallas_call(
        project_kernel,
        in_specs=[vmem] * 3 + [pl.BlockSpec(memory_space=pl.ANY)],
        out_specs=vmem,
        out_shape=jax.ShapeDtypeStruct((128, 8, 128), F32),
        scratch_shapes=[
            pltpu.VMEM((MG * ROWS, 512), BF),
            pltpu.VMEM((pair.shape[0], 64), BF),
            pltpu.VMEM((64, pair.shape[1]), F32),
            pltpu.VMEM(pair.shape, BF),
            pltpu.SemaphoreType.DMA((pair.shape[0] // WIDE,)),
        ],
        compiler_params=pltpu.CompilerParams(vmem_limit_bytes=44 * 2**20),
        name="project",
    )(got, const(tab["unswap"]), const(tab["back"]), pair)


def parts_of(device):
    grid, vec = device // 8, device % 8
    return grid // 4, (vec // 4) * 2 + (grid // 2) % 2, grid % 2, vec % 4


def device_at(z, x, core, y):
    return (z * 4 + (x % 2) * 2 + core) * 8 + (x // 2) * 4 + y


def bring(data, dz=0, dx=0, dcore=0, dy=0):
    pairs = []
    for device in range(128):
        z, x, core, y = parts_of(device)
        source = device_at((z + dz) % 4, (x + dx) % 4, (core + dcore) % 2, (y + dy) % 4)
        pairs.append((source, device))
    return lax.ppermute(data, AXES, pairs)


def fill(base, blocks, slot, more, held, out):
    start = 0
    for block in blocks:
        rows = block.shape[0]
        held[start : start + rows, :] = block[...]
        start += rows
    chunk = 256
    for first in range(0, slot.shape[1], chunk):
        wanted = slot[:, first : first + chunk]
        picks = []
        for block, number in zip(blocks, base):
            index = lax.broadcasted_iota(jnp.int32, (block.shape[0], chunk), 0) + number
            picks.append(jnp.where(index == wanted, 1.0, 0.0).astype(BF))
        total = lax.dot_general(
            held[...],
            jnp.concatenate(picks, axis=0),
            (((0,), (0,)), ((), ())),
            preferred_element_type=F32,
        )
        if more:
            total = total + more[0][:, first : first + chunk].astype(F32)
        out[:, first : first + chunk] = total.astype(BF)


def place_kernel(count, base, *refs):
    blocks, (slot, *more), (out, held) = refs[:count], refs[count:-2], refs[-2:]
    fill(base, blocks, slot, more, held, out)


def place(slot, blocks, base, more=()):
    vmem = pl.BlockSpec(memory_space=pltpu.VMEM)
    norb, npts = blocks[0].shape[1], slot.shape[1]
    slots = sum(block.shape[0] for block in blocks)
    return pl.pallas_call(
        functools.partial(place_kernel, len(blocks), base),
        in_specs=[vmem] * (1 + len(blocks) + len(more)),
        out_specs=vmem,
        out_shape=jax.ShapeDtypeStruct((norb, npts), BF),
        scratch_shapes=[pltpu.VMEM((slots, norb), BF)],
        compiler_params=pltpu.CompilerParams(vmem_limit_bytes=20 * 2**20),
        cost_estimate=pl.CostEstimate(
            flops=2 * slots * norb * npts, bytes_accessed=4 * norb * npts, transcendentals=0
        ),
        name="place",
    )(*blocks, slot, *more)


def summed_rows(orbitals, points, me):
    row_count = orbitals.shape[0]
    local_pos = points - me * row_count
    inside = (local_pos >= 0) & (local_pos < row_count)
    picked = jnp.take(orbitals, jnp.clip(local_pos, 0, row_count - 1), axis=0)
    picked = jnp.where(inside[:, None], picked, jnp.zeros_like(picked)).astype(F32)
    return lax.psum(picked, AXES).astype(BF).T


def owners(points, row_count):
    return ((points.astype(F32) + 0.5) * (1.0 / row_count)).astype(jnp.int32)


def ranks(label, labels):
    size = 256
    shape = (size, size)
    early = lax.broadcasted_iota(jnp.int32, shape, 0) < lax.broadcasted_iota(jnp.int32, shape, 1)
    early = jnp.where(early, 1.0, 0.0).astype(BF)
    index = lax.broadcasted_iota(jnp.int32, (labels, size), 0)
    seen = jnp.zeros((labels, 1), F32)
    found = []
    for first in range(0, label.shape[1], size):
        match = jnp.where(index == label[:, first : first + size], 1.0, 0.0)
        before = mm(match.astype(BF), early) + seen
        found.append(jnp.sum(match * before, axis=0, keepdims=True))
        seen = seen + jnp.sum(match, axis=1, keepdims=True)
    return jnp.concatenate(found, axis=1).astype(jnp.int32), jnp.max(seen)


def lookup(key, value, first, rows):
    number = lax.broadcasted_iota(jnp.int32, (rows, 128), 0) + first
    total = jnp.zeros((rows, 128), jnp.int32)
    for start in range(0, key.shape[1], 128):
        total = total + jnp.where(
            key[:, start : start + 128] == number, value[:, start : start + 128], 0
        )
    return jnp.sum(total.astype(F32), axis=1, keepdims=True).astype(jnp.int32)


def own_kernel(me, points, orbitals, own, rank, picks, spots, near, sems, one):
    row_count = orbitals.shape[0]
    owner = owners(points[...], row_count)
    mine = owner == me[0]
    own_rank, _ = ranks(jnp.where(mine, 0, 16), 16)
    key = jnp.where(mine, own_rank, -1)
    pick = lookup(key, points[...] - me[0] * row_count, 0, ROOM)
    picks[...] = jnp.broadcast_to(pick, (ROOM, 128))
    move = pltpu.make_async_copy(picks, spots, one)
    move.start()
    move.wait()
    copies = []
    for place in range(ROOM):
        start = pl.multiple_of((spots[place, 0] >> 4) << 4, 16)
        copies.append(
            pltpu.make_async_copy(
                orbitals.at[pl.ds(start, 16), :],
                near.at[pl.ds(place * 16, 16), :],
                sems.at[place],
            )
        )
        copies[-1].start()
    rank[...] = owner
    for copy in copies:
        copy.wait()
    lane = lax.broadcasted_iota(jnp.int32, (ROOM, 16 * ROOM), 1)
    line = lax.broadcasted_iota(jnp.int32, (ROOM, 16 * ROOM), 0)
    select = jnp.where(lane == line * 16 + (pick & 15), 1.0, 0.0).astype(BF)
    own[...] = mm(select, near[...]).astype(BF)


def index_kernel(me, owner_of, fits, choose, slot):
    _, my_x, my_core, _ = parts_of(me[0])
    owner = owner_of[...]
    z, y, core = owner >> 5, owner & 3, (owner >> 3) & 1
    x = ((owner >> 2) & 1) * 2 + ((owner >> 4) & 1)
    own_rank, own_most = ranks(owner, 128)
    group_rank, group_most = ranks(x * 2 + core, 16)
    fit = (own_most <= ROOM) & (group_most <= GROUP)
    fits[0] = fit.astype(jnp.int32)
    spot = z * (4 * ROOM) + y * ROOM + own_rank
    key = jnp.where((x == my_x) & (core == my_core), group_rank, -1)
    for first in range(0, GROUP, 64):
        source = lookup(key, spot + 1, first, 64) - 1
        lane = lax.broadcasted_iota(jnp.int32, (64, 16 * ROOM), 1)
        choose[first : first + 64, :] = jnp.where(source == lane, 1.0, 0.0).astype(BF)
    number = (((core - my_core) & 1) * 4 + ((x - my_x) & 3)) * GROUP + group_rank
    slot[...] = jnp.where(fit, number, -1)


def fetch_own(me, points, orbitals):
    vmem = pl.BlockSpec(memory_space=pltpu.VMEM)
    smem = pl.BlockSpec(memory_space=pltpu.SMEM)
    npts, norb = points.shape[0], orbitals.shape[1]
    return pl.pallas_call(
        own_kernel,
        in_specs=[smem, vmem, pl.BlockSpec(memory_space=pl.ANY)],
        out_specs=[vmem, vmem],
        out_shape=[
            jax.ShapeDtypeStruct((ROOM, norb), BF),
            jax.ShapeDtypeStruct((1, npts), jnp.int32),
        ],
        scratch_shapes=[
            pltpu.VMEM((ROOM, 128), jnp.int32),
            pltpu.SMEM((ROOM, 128), jnp.int32),
            pltpu.VMEM((16 * ROOM, norb), BF),
            pltpu.SemaphoreType.DMA((ROOM,)),
            pltpu.SemaphoreType.DMA,
        ],
        compiler_params=pltpu.CompilerParams(vmem_limit_bytes=16 * 2**20),
        name="own",
    )(me.reshape(1), points[None], orbitals)


def index(me, owner):
    vmem = pl.BlockSpec(memory_space=pltpu.VMEM)
    smem = pl.BlockSpec(memory_space=pltpu.SMEM)
    return pl.pallas_call(
        index_kernel,
        in_specs=[smem, vmem],
        out_specs=[smem, vmem, vmem],
        out_shape=[
            jax.ShapeDtypeStruct((1,), jnp.int32),
            jax.ShapeDtypeStruct((GROUP, 16 * ROOM), BF),
            jax.ShapeDtypeStruct(owner.shape, jnp.int32),
        ],
        compiler_params=pltpu.CompilerParams(vmem_limit_bytes=16 * 2**20),
        cost_estimate=pl.CostEstimate(
            flops=3 * 10**9, bytes_accessed=10**7, transcendentals=0
        ),
        name="index",
    )(me.reshape(1), owner)


def spread_rows(held, slot):
    mate = lambda block: bring(block, dcore=1)
    half, ring = GROUP // 2, 4 * GROUP
    right, left = bring(held, dx=1), bring(held, dx=3)
    rows = place(slot, [held, mate(held)], (0, ring))
    far_a, far_b = bring(right[:half], dx=1), bring(left[half:], dx=3)
    near = [right, left, mate(right), mate(left)]
    rows = place(slot, near, (GROUP, 3 * GROUP, ring + GROUP, ring + 3 * GROUP), (rows,))
    far_a, far_b, rows = lax.optimization_barrier((far_a, far_b, rows))
    return rows, far_a, far_b, mate(far_a), mate(far_b)


def gather_rows(orbitals, points, me):
    own, owner = fetch_own(me, points, orbitals)
    copies = jnp.broadcast_to(own[None], (16,) + own.shape)
    square = lax.all_to_all(copies, ("z", "y"), 0, 0).reshape(16 * ROOM, own.shape[1])
    fits, choose, slot = index(me, owner)
    shape = (orbitals.shape[1], points.shape[0])
    spare = lax.cond(
        fits[0] > 0,
        lambda: jnp.zeros(shape, BF),
        lambda: summed_rows(orbitals, points, me),
    )
    square, _ = lax.optimization_barrier((square, spare[:8, :128]))
    held = mm(choose, square).astype(BF)
    rows, *far = spread_rows(held, slot)
    return fits, spare, rows, slot, far


def shards(orbitals, inverse_panel, points):
    tab = tables()
    devices = lax.axis_size(AXES)
    me = lax.axis_index(AXES)
    npoints, cols = inverse_panel.shape
    fits, spare, part_t, slot, far = gather_rows(orbitals, points, me)
    panel2 = jnp.concatenate([inverse_panel, inverse_panel], axis=1)
    pair, send = make_pairs(fits, spare, orbitals, part_t, slot, far, panel2, tab)
    planes = lax.all_to_all(send.reshape(devices, ROWS, 128), AXES, 0, 0)
    ret = solve(me.reshape(1), planes.reshape(devices * ROWS, 128), tab)
    got = lax.all_to_all(ret.reshape(devices, ROWS, 128), AXES, 0, 0)
    parts = project(got.reshape(MG, CG, ROWS, 128), pair, tab)
    parts = lax.all_to_all(parts, AXES, 0, 0)
    total = jnp.sum(parts, axis=0)
    return jnp.concatenate([total[:, :cols], total[:, cols:]], axis=0)


def solution(mesh):
    fine = jax.sharding.Mesh(mesh.devices.reshape(4, 2, 2, 2, 4), AXES)
    in_specs = (P(AXES, None), P(), P())
    return jax.shard_map(
        shards, mesh=fine, in_specs=in_specs, out_specs=P(AXES, None), check_vma=False
    )
```
